256 devices in a mesh: row: 32 (over y, x, core), col: 8 (over z).
Axes of the slice: x: 4, y: 4, z: 8, core: 2. Of those that a mesh axis runs over, the one named last changes fastest.
Arguments:
- factor: bfloat16 [256, 32, 128, 128], P('row', 'col'), may hold values from -0.1796875 to 0.1796875
- inverse_pivot: float32 [256, 128], P('row'), may hold values from 0.5 to 2
- lower_rhs: float32 [16, 256, 128], P(None, 'col'), may hold values from -6 to 6
- upper_rhs: float32 [16, 256, 128], P(None, 'col'), may hold values from -6 to 6
- snode_of_block: int32 [256], replicated, may hold values from 0 to 63, as said below
- level_of_snode: int32 [64], replicated, may hold values from 0 to 5, as said below
- slot_columns: int32 [256, 32], P('row', 'col'), may hold values from 0 to 256, as said below
Outputs:
- lower_solution: float32 [16, 256, 128], P(None, 'row')
- upper_solution: float32 [16, 256, 128], P(None, 'row')
The draws below stay inside these ranges and needn't reach their ends.
Inputs may be any that keep to these rules, and one draw needn't show every extreme that they name: `snode_of_block`: never falling along the blocks, starting at 0 and rising by at most one; every supernode covers an even number of blocks. `level_of_snode`: never falling along the supernodes, starting at 0 and rising by at most one; every level holds one or more supernodes, the top level exactly one, the last. `slot_columns`: the slots of process column c name distinct blocks J with J % 8 == c, or 256; every block row names its own block; a named J lies in the row's supernode or in one that is an ancestor or descendant of it in the elimination tree, in which every supernode below the top level has its parent one level up; some block row fills all 4 slots of some process column.
All inputs are finite; a program needn't handle non-finite values.
Results may differ from the reference program's by a relative error of at most 0.0059.
Values may be sent and summed in bfloat16 or wider, within the bound.
A program may use at most 128 MiB of HBM per device.

```python
import math
import jax
import jax.numpy as jnp
from jax import lax

B = 128
BR = 8
KC = 4
NRHS = 16
NB = 256
BC = 32
SNODES = 64
LEVELS = 6
N_COL = 8


def structure(key):
    base_key = jax.random.fold_in(key, 41)
    cut_key, level_key, parent_key, coin_key, score_key = jax.random.split(base_key, 5)
    pair_count = NB // 2
    cut_rank = jax.random.permutation(cut_key, pair_count - 1)
    cut_flags = (cut_rank < SNODES - 1).astype(jnp.int32)
    pair_snode = jnp.concatenate([jnp.zeros((1,), jnp.int32), jnp.cumsum(cut_flags).astype(jnp.int32)])
    block_snode = jnp.repeat(pair_snode, 2).astype(jnp.int32)
    level_rank = jax.random.permutation(level_key, SNODES - 2)
    level_flags = (level_rank < LEVELS - 2).astype(jnp.int32)
    lower_levels = jnp.concatenate([jnp.zeros((1,), jnp.int32), jnp.cumsum(level_flags).astype(jnp.int32)])
    snode_level = jnp.concatenate([lower_levels, jnp.full((1,), LEVELS - 1, jnp.int32)])
    level_ids = jnp.arange(LEVELS, dtype=jnp.int32)
    member = (snode_level[:, None] == level_ids[None, :]).astype(jnp.int32)
    level_sizes = jnp.sum(member, axis=0).astype(jnp.int32)
    level_starts = (jnp.cumsum(level_sizes) - level_sizes).astype(jnp.int32)
    next_level = jnp.minimum(snode_level + 1, LEVELS - 1)
    next_onehot = (next_level[:, None] == level_ids[None, :]).astype(jnp.int32)
    next_size = jnp.sum(next_onehot * level_sizes[None, :], axis=1).astype(jnp.int32)
    next_start = jnp.sum(next_onehot * level_starts[None, :], axis=1).astype(jnp.int32)
    random_picks = jax.random.randint(parent_key, (SNODES,), 0, 1 << 20).astype(jnp.int32)
    parent = next_start + random_picks % next_size
    has_parent = snode_level < LEVELS - 1
    snode_ids = jnp.arange(SNODES, dtype=jnp.int32)
    step_matrix = ((snode_ids[None, :] == parent[:, None]) & has_parent[:, None]).astype(jnp.int32)
    ancestors = step_matrix
    reached = step_matrix
    for distance in range(LEVELS - 2):
        reached = (jnp.dot(reached, step_matrix) > 0).astype(jnp.int32)
        ancestors = jnp.maximum(ancestors, reached)
    related = jnp.maximum(ancestors, ancestors.T)
    block_related = related[block_snode][:, block_snode]
    coin_flips = jax.random.randint(coin_key, (NB, NB), 0, 2).astype(jnp.int32)
    block_ids = jnp.arange(NB, dtype=jnp.int32)
    coin_flips = jnp.where(block_ids[:, None] < block_ids[None, :], coin_flips, coin_flips.T)
    is_root = block_snode == SNODES - 1
    coin_flips = jnp.where(is_root[:, None] | is_root[None, :], 1, coin_flips)
    same_snode = block_snode[:, None] == block_snode[None, :]
    candidate = jnp.where(same_snode, 1, block_related * coin_flips).astype(jnp.int32)
    diag = (block_ids[:, None] == block_ids[None, :]).astype(jnp.int32)
    big = NB * NB
    tie_break = jax.random.permutation(score_key, big).astype(jnp.int32).reshape(NB, NB)
    score = candidate * (4 * big) + diag * (2 * big) + same_snode.astype(jnp.int32) * big + tie_break
    by_class = jnp.transpose(score.reshape(NB, BC, N_COL), (0, 2, 1))
    cand_class = jnp.transpose(candidate.reshape(NB, BC, N_COL), (0, 2, 1))
    chosen_score, chosen = lax.top_k(by_class, KC)
    chosen = chosen.astype(jnp.int32)
    chosen_cand = jnp.take_along_axis(cand_class, chosen, axis=2)
    class_ids = jnp.arange(N_COL, dtype=jnp.int32)
    natural = chosen * N_COL + class_ids[None, :, None]
    slots = jnp.where(chosen_cand > 0, natural, NB).astype(jnp.int32).reshape(NB, N_COL * KC)
    row_order = (block_ids % BR * (NB // BR) + block_ids // BR).astype(jnp.int32)
    return (block_snode, snode_level, jnp.take(slots, row_order, axis=0).astype(jnp.int32))


def draw_snode_of_block(key, part):
    return structure(key)[0]


def draw_level_of_snode(key, part):
    return structure(key)[1]


def draw_slot_columns(key, part):
    return structure(key)[2]


def steps_of(own_key, dims, shards, smallest, largest):
    gain, own = 1.0, jax.random.fold_in(own_key, 6)
    for dim, shards_of in shards:
        heights = jnp.exp(jax.random.uniform(jax.random.fold_in(own, dim), (shards_of,), jnp.float32, smallest / len(shards), largest / len(shards)))
        gain = gain * jnp.repeat(heights, dims[dim] // shards_of).reshape([-1 if axis == dim else 1 for axis in range(len(dims))])
    return gain


def scatter_about(rng, dims, scale, most, cuts=(), kind=jnp.bfloat16):
    result = jax.random.normal(rng, dims, jnp.float32) * scale
    if len(cuts) > 0:
        result = steps_of(rng, dims, cuts, -0.22, 0.18) * result
    return jnp.clip(result, min=-most, max=most).astype(kind)


def setup_inputs(seed: int = 0) -> dict:
    keys = jax.random.split(jax.random.key(seed), 8)
    return {
        "factor": scatter_about(keys[0], (NB, N_COL * KC, B, B), 0.03, 0.1796875, ((0, 32), (1, 8))),
        "inverse_pivot": jnp.clip(jnp.exp(math.log(2.0) - 1.3862944 * jax.random.uniform(keys[1], (NB, B), jnp.float32) ** steps_of(keys[1], (NB, B), ((0, 32),), -0.2, 0.2)), 0.5, 2.0),
        "lower_rhs": scatter_about(keys[2], (NRHS, NB, B), 1.0, 6.0, ((1, 8),), jnp.float32),
        "upper_rhs": scatter_about(keys[3], (NRHS, NB, B), 1.0, 6.0, ((1, 8),), jnp.float32),
        "snode_of_block": draw_snode_of_block(jax.random.fold_in(keys[7], 71), 0),
        "level_of_snode": draw_level_of_snode(jax.random.fold_in(keys[7], 71), 0),
        "slot_columns": draw_slot_columns(jax.random.fold_in(keys[7], 71), 0),
    }


def block_levels(snode_of_block, level_of_snode):
    onehot = snode_of_block[:, None] == jnp.arange(SNODES, dtype=jnp.int32)[None, :]
    return jnp.sum(jnp.where(onehot, level_of_snode[None, :], 0), axis=1).astype(jnp.int32)


def column_position(block):
    return ((block % N_COL) * BC + block // N_COL).astype(jnp.int32)


def reference(factor, inverse_pivot, lower_rhs, upper_rhs, snode_of_block, level_of_snode, slot_columns):
    row_count = NB // BR
    col_count = NB // BC
    blocks = jnp.arange(NB, dtype=jnp.int32)
    levels = block_levels(snode_of_block, level_of_snode)
    col_blocks = ((blocks % BC) * col_count + blocks // BC).astype(jnp.int32)
    row_blocks = ((blocks % BR) * row_count + blocks // BR).astype(jnp.int32)
    col_levels = levels[col_blocks]
    strict_low = jnp.tril(jnp.ones((B, B), jnp.float32), -1)
    strict_up = jnp.triu(jnp.ones((B, B), jnp.float32), 1)
    high = lax.Precision.HIGHEST

    def products(lower_in, upper_in):
        lower_f = lower_in.astype(jnp.float32)
        upper_f = upper_in.astype(jnp.float32)

        def row_terms(row_block):
            position = ((row_block % row_count) * BR + row_block // row_count).astype(jnp.int32)
            row_panel = lax.dynamic_index_in_dim(factor, position, 0, keepdims=False).astype(jnp.float32)
            slot_ids = lax.dynamic_index_in_dim(slot_columns, position, 0, keepdims=False)
            valid = slot_ids < NB
            safe = jnp.minimum(slot_ids, NB - 1).astype(jnp.int32)
            own_snode = lax.dynamic_index_in_dim(snode_of_block, row_block, 0, keepdims=False)
            own_level = lax.dynamic_index_in_dim(levels, row_block, 0, keepdims=False)
            same = jnp.take(snode_of_block, safe) == own_snode
            slot_level = jnp.take(levels, safe)
            lower_s = valid & jnp.where(same, safe < row_block, own_level > slot_level)
            upper_s = valid & jnp.where(same, safe > row_block, own_level < slot_level)
            diag_s = valid & (safe == row_block)
            lower_w = jnp.where(diag_s[:, None, None], strict_low[None], lower_s.astype(jnp.float32)[:, None, None])
            upper_w = jnp.where(diag_s[:, None, None], strict_up[None], upper_s.astype(jnp.float32)[:, None, None])
            places = column_position(safe)
            lower_pick = jnp.take(lower_f, places, axis=1)
            upper_pick = jnp.take(upper_f, places, axis=1)
            lower_terms = jnp.einsum("ksj,sij->ki", lower_pick, row_panel * lower_w, precision=high)
            upper_terms = jnp.einsum("ksj,sij->ki", upper_pick, row_panel * upper_w, precision=high)
            own_place = column_position(row_block)
            lower_own = lax.dynamic_index_in_dim(lower_f, own_place, 1, keepdims=False)
            upper_own = lax.dynamic_index_in_dim(upper_f, own_place, 1, keepdims=False)
            pivot_row = lax.dynamic_index_in_dim(inverse_pivot, position, 0, keepdims=False)
            return lower_terms + lower_own, upper_terms + pivot_row[None, :] * upper_own

        lower_all, upper_all = lax.map(row_terms, blocks)
        return jnp.transpose(lower_all, (1, 0, 2)), jnp.transpose(upper_all, (1, 0, 2))

    lower_res = lower_rhs
    upper_res = upper_rhs
    lower_sol = jnp.zeros((NRHS, NB, B), jnp.float32)
    upper_sol = jnp.zeros((NRHS, NB, B), jnp.float32)
    for level_step in range(LEVELS):
        lower_level = level_step
        upper_level = LEVELS - 1 - level_step
        lower_in = jnp.where((col_levels == lower_level)[None, :, None], lower_res, 0.0).astype(jnp.bfloat16)
        upper_in = jnp.where((col_levels == upper_level)[None, :, None], upper_res, 0.0).astype(jnp.bfloat16)
        lower_sum, upper_sum = products(lower_in, upper_in)
        lower_new = jnp.where((levels == lower_level)[None, :, None], lower_sum, 0.0)
        upper_new = jnp.where((levels == upper_level)[None, :, None], upper_sum, 0.0)
        lower_sol = lower_sol + lower_new
        upper_sol = upper_sol + upper_new
        if level_step + 1 < LEVELS:
            lower_upd, upper_upd = products(lower_new.astype(jnp.bfloat16)[:, col_blocks], upper_new.astype(jnp.bfloat16)[:, col_blocks])
            lower_back = jnp.where((levels > lower_level)[None, :, None], lower_upd, 0.0).astype(jnp.bfloat16)
            upper_back = jnp.where((levels < upper_level)[None, :, None], upper_upd, 0.0).astype(jnp.bfloat16)
            lower_res = lower_res - lower_back[:, col_blocks].astype(jnp.float32)
            upper_res = upper_res - upper_back[:, col_blocks].astype(jnp.float32)
    return lower_sol[:, row_blocks], upper_sol[:, row_blocks]
```

```python
import functools

import jax
import jax.numpy as jnp
from jax import lax
from jax.experimental import pallas as pl
from jax.experimental.pallas import tpu as pltpu
from jax.sharding import PartitionSpec as P

MESH = pl.DeviceIdType.MESH
LEVELS = 6
ROUNDS = 2 * LEVELS - 1
NT = (((1,), (1,)), ((), ()))


def kernel(
    dims, tbl, flt, f_ref, v0_ref, own_ref, piv_ref, low_ref, up_ref,
    f2, held, land, psend, precv, xs, xrecv, send1, recv1, send2, recv2, send3, recv3,
):
    rows, cols, nrow, nslot, ncol = dims
    per = rows // cols
    zero = ROUNDS * ncol
    n_tbl = ROUNDS * nrow * nslot
    row, col = lax.axis_index("row"), lax.axis_index("col")
    base, lane = (row // cols) * cols, row % cols
    on_diag = col == lane
    own_pos = row // cols + per * (row % cols)

    def dest(i):
        return (base + i, lane)

    def source(c):
        return (base + col, c)

    barrier = pltpu.get_barrier_semaphore()

    def plane(body):
        def step(k, carry):
            body(lax.rem(row + k, rows))
            return carry

        lax.fori_loop(1, rows, step, 0)

    def across(body):
        def step(k, carry):
            i = lax.rem(col + k, cols)
            mine = jnp.logical_and(on_diag, i == col)
            body(i, mine)
            return carry

        lax.fori_loop(0, cols, step, 0)

    plane(lambda to: pl.semaphore_signal(barrier, inc=1, device_id=(to, col), device_id_type=MESH))

    def greet(i, mine):
        @pl.when(jnp.logical_not(mine))
        def _():
            pl.semaphore_signal(barrier, inc=1, device_id=dest(i), device_id_type=MESH)
            pl.semaphore_signal(barrier, inc=1, device_id=source(i), device_id_type=MESH)

    across(greet)

    r_id = lax.broadcasted_iota(jnp.int32, f_ref.shape[1:], 0)
    c_id = lax.broadcasted_iota(jnp.int32, f_ref.shape[1:], 1)
    below = (c_id < r_id).astype(jnp.float32)
    above = (c_id > r_id).astype(jnp.float32)

    def mask_block(b, carry):
        block = f_ref[b].astype(jnp.float32)
        d = flt[n_flt_diag + b]
        f2[b] = (block * (1.0 - d + d * below)).astype(jnp.bfloat16)
        f2[nrow * nslot + b] = (block * (1.0 - d + d * above)).astype(jnp.bfloat16)
        return carry

    n_flt_diag = ROUNDS * (2 * nrow + 2)
    lax.fori_loop(0, nrow * nslot, mask_block, 0)
    held[pl.ds(0, ncol)] = v0_ref[...]
    held[zero] = jnp.zeros(held.shape[1:], held.dtype)
    xs[...] = jnp.zeros_like(xs)

    n_in = jnp.where(on_diag, 2 * (cols - 1), 2 * cols) + rows - 1
    pl.semaphore_wait(barrier, n_in)

    def reduce_round(n, with_own):
        for i in range(nrow):
            acc = None
            sel = tbl[n_tbl + n * nrow + i] * (nrow * nslot)
            for s in range(nslot):
                b = i * nslot + s
                term = lax.dot_general(
                    held[tbl[n * (nrow * nslot) + b]], f2[sel + b], NT,
                    preferred_element_type=jnp.float32,
                )
                acc = term if acc is None else acc + term
            if with_own:
                at = n * ncol + row // cols + per * i
                cl = flt[(n * nrow + i) * 2]
                cu = flt[(n * nrow + i) * 2 + 1]
                acc = acc + (cl + cu * piv_ref[pl.ds(i, 1), :]) * held[at].astype(jnp.float32)
            psend[n, i] = acc

            mine = jnp.logical_and(on_diag, col == i)

            @pl.when(jnp.logical_not(mine))
            def _():
                pltpu.make_async_remote_copy(
                    src_ref=psend.at[n, i], dst_ref=precv.at[n, col],
                    send_sem=send1.at[n], recv_sem=recv1.at[n],
                    device_id=dest(i), device_id_type=MESH,
                ).start()

            @pl.when(mine)
            def _():
                precv[n, col] = acc

        @pl.when(on_diag)
        def _():
            pltpu.make_async_copy(
                precv.at[n, pl.ds(0, cols - 1)], precv.at[n, pl.ds(0, cols - 1)], recv1.at[n]
            ).wait()

        @pl.when(jnp.logical_not(on_diag))
        def _():
            pltpu.make_async_copy(precv.at[n], precv.at[n], recv1.at[n]).wait()

        total = precv[n, 0]
        for c in range(1, cols):
            total = total + precv[n, c]
        return total

    def spread(n, value):
        land[n, own_pos] = value.astype(jnp.bfloat16)

        def send(to):
            pltpu.make_async_remote_copy(
                src_ref=land.at[n, own_pos], dst_ref=land.at[n, own_pos],
                send_sem=send2.at[n], recv_sem=recv2.at[n],
                device_id=(to, col), device_id_type=MESH,
            ).start()

        plane(send)
        some = land.at[n, pl.ds(0, rows - 1)]
        pltpu.make_async_copy(some, some, recv2.at[n]).wait()
        held[pl.ds((n + 1) * ncol, ncol)] = land[n]

    n_own = ROUNDS * 2 * nrow

    def solve(n):
        y = reduce_round(n, True)
        xs[0] += flt[n_own + 2 * n] * y
        xs[1] += flt[n_own + 2 * n + 1] * y
        return y

    def level(t, carry):
        n = 2 * t
        spread(n, solve(n))
        w = reduce_round(n + 1, False)
        v = flt[n_own + 2 * n + 2] * own_ref[0] + flt[n_own + 2 * n + 3] * own_ref[1] - w
        spread(n + 1, v)
        return carry

    lax.fori_loop(0, LEVELS - 1, level, 0)
    solve(ROUNDS - 1)

    place = row % cols

    def give(c, mine):
        @pl.when(jnp.logical_not(mine))
        def _():
            pltpu.make_async_remote_copy(
                src_ref=xs, dst_ref=xrecv.at[place], send_sem=send3, recv_sem=recv3,
                device_id=source(c), device_id_type=MESH,
            ).start()

        @pl.when(mine)
        def _():
            xrecv[place] = xs[...]

    across(give)

    def drain(n, carry):
        @pl.when(on_diag)
        def _():
            part = psend.at[n, pl.ds(0, cols - 1)]
            pltpu.make_async_copy(part, part, send1.at[n]).wait()

        @pl.when(jnp.logical_not(on_diag))
        def _():
            pltpu.make_async_copy(psend.at[n], psend.at[n], send1.at[n]).wait()

        return carry

    lax.fori_loop(0, ROUNDS, drain, 0)

    def drain2(n, carry):
        some = land.at[n, pl.ds(0, rows - 1)]
        pltpu.make_async_copy(some, some, send2.at[n]).wait()
        return carry

    lax.fori_loop(0, ROUNDS - 1, drain2, 0)

    @pl.when(on_diag)
    def _():
        part = xrecv.at[pl.ds(0, cols - 1)]
        pltpu.make_async_copy(part, part, recv3).wait()
        pltpu.make_async_copy(part, part, send3).wait()

    @pl.when(jnp.logical_not(on_diag))
    def _():
        pltpu.make_async_copy(xrecv, xrecv, recv3).wait()
        pltpu.make_async_copy(xrecv, xrecv, send3).wait()

    for i in range(nrow):
        low_ref[:, i, :] = xrecv[i, 0]
        up_ref[:, i, :] = xrecv[i, 1]


def shards(factor, inverse_pivot, lower_rhs, upper_rhs, snode_of_block, level_of_snode, slot_columns):
    rows, cols = lax.axis_size("row"), lax.axis_size("col")
    row, col = lax.axis_index("row"), lax.axis_index("col")
    nrow, nslot, size = factor.shape[:3]
    nrhs, ncol = lower_rhs.shape[:2]
    total = snode_of_block.shape[0]
    i32, f32 = jnp.int32, jnp.float32
    zero = ROUNDS * ncol

    ids = jnp.arange(total, dtype=i32)
    hot = snode_of_block[:, None] == jnp.arange(level_of_snode.shape[0], dtype=i32)[None, :]
    levels = jnp.sum(jnp.where(hot, level_of_snode[None, :], 0), axis=1)

    def look(table, at):
        return jnp.sum(jnp.where(at[..., None] == ids, table, 0), axis=-1)

    row_ids = jnp.arange(nrow, dtype=i32) * rows + row
    col_ids = jnp.arange(ncol, dtype=i32) * cols + col
    own_id = (row // cols) * cols + col + rows * (row % cols)
    row_level, row_snode = look(levels, row_ids), look(snode_of_block, row_ids)
    col_level, own_level = look(levels, col_ids), look(levels, own_id)
    slot_level, slot_snode = look(levels, slot_columns), look(snode_of_block, slot_columns)
    valid = slot_columns < total
    same = valid & (slot_snode == row_snode[:, None])
    other = valid & (slot_snode != row_snode[:, None])
    diag = slot_columns == row_ids[:, None]
    place = slot_columns // cols
    lo_in = (same & (slot_columns < row_ids[:, None])) | diag
    up_in = (same & (slot_columns > row_ids[:, None])) | diag
    lo_out = other & (row_level[:, None] > slot_level)
    up_out = other & (row_level[:, None] < slot_level)
    top = LEVELS - 1

    n = jnp.arange(ROUNDS, dtype=i32)
    t = n // 2
    inside = (n % 2 == 0)[:, None, None]
    at = (t + n % 2)[:, None]
    is_lo, is_up = row_level[None] == at, row_level[None] == top - at
    in_pick = n[:, None, None] * ncol + place[None]
    lo_pick = jnp.where(inside, in_pick, (2 * slot_level[None] + 1) * ncol + place[None])
    up_pick = jnp.where(inside, in_pick, (2 * (top - slot_level[None]) + 1) * ncol + place[None])
    lo_on = is_lo[:, :, None] & jnp.where(inside, lo_in[None], lo_out[None])
    up_on = is_up[:, :, None] & jnp.where(inside, up_in[None], up_out[None])
    picks = jnp.where(lo_on, lo_pick, jnp.where(up_on, up_pick, zero))
    tbl = jnp.concatenate([picks.reshape(-1), is_up.astype(i32).reshape(-1)])

    on_diag = row % cols == col
    own_w = jnp.stack([is_lo & on_diag, is_up & on_diag], axis=-1).astype(f32)
    mine = jnp.stack([own_level == at[:, 0], own_level == top - at[:, 0]], axis=-1).astype(f32)
    flt = jnp.concatenate([own_w.reshape(-1), mine.reshape(-1), diag.astype(f32).reshape(-1)])

    first = jnp.where((col_level == 0)[None, :, None], lower_rhs, 0.0) + jnp.where(
        (col_level == top)[None, :, None], upper_rhs, 0.0
    )
    v0 = jnp.transpose(first.astype(jnp.bfloat16), (1, 0, 2))
    own_pos = row // cols + (rows // cols) * (row % cols)
    own = jnp.stack([
        lax.dynamic_index_in_dim(lower_rhs, own_pos, 1, keepdims=False),
        lax.dynamic_index_in_dim(upper_rhs, own_pos, 1, keepdims=False),
    ])

    vmem, smem = pl.BlockSpec(memory_space=pltpu.VMEM), pl.BlockSpec(memory_space=pltpu.SMEM)
    dma = pltpu.SemaphoreType.DMA
    blocks = nrow * nslot
    return pl.pallas_call(
        functools.partial(kernel, (rows, cols, nrow, nslot, ncol)),
        out_shape=[jax.ShapeDtypeStruct((nrhs, nrow, size), f32)] * 2,
        in_specs=[smem, smem, vmem, vmem, vmem, vmem],
        out_specs=[vmem, vmem],
        scratch_shapes=[
            pltpu.VMEM((2 * blocks, size, size), jnp.bfloat16),
            pltpu.VMEM((zero + 1, nrhs, size), jnp.bfloat16),
            pltpu.VMEM((ROUNDS - 1, ncol, nrhs, size), jnp.bfloat16),
            pltpu.VMEM((ROUNDS, nrow, nrhs, size), f32),
            pltpu.VMEM((ROUNDS, cols, nrhs, size), f32),
            pltpu.VMEM((2, nrhs, size), f32),
            pltpu.VMEM((nrow, 2, nrhs, size), f32),
            dma((ROUNDS,)), dma((ROUNDS,)), dma((ROUNDS - 1,)), dma((ROUNDS - 1,)), dma, dma,
        ],
        compiler_params=pltpu.CompilerParams(
            collective_id=0, has_side_effects=True, vmem_limit_bytes=32 * 2**20
        ),
        cost_estimate=pl.CostEstimate(
            flops=2 * ROUNDS * blocks * size * size * nrhs,
            bytes_accessed=4 * blocks * size * size, transcendentals=0,
        ),
    )(tbl, flt, factor.reshape(blocks, size, size), v0, own, inverse_pivot)


def solution(mesh):
    in_specs = (
        P("row", "col", None, None),
        P("row", None),
        P(None, "col", None),
        P(None, "col", None),
        P(),
        P(),
        P("row", "col"),
    )
    out_specs = (P(None, "row", None), P(None, "row", None))
    return jax.shard_map(shards, mesh=mesh, in_specs=in_specs, out_specs=out_specs, check_vma=False)
```

```python
import functools

import jax
import jax.numpy as jnp
from jax import lax
from jax.experimental import pallas as pl
from jax.experimental.pallas import tpu as pltpu
from jax.sharding import PartitionSpec as P

MESH = pl.DeviceIdType.MESH
LEVELS = 6
TOP = LEVELS - 1
ROUNDS = 2 * LEVELS - 1
NT = (((1,), (1,)), ((), ()))
SIDE, CORES = 4, 2
FAR = 4096


def ring(d, n):
    return min(d % n, -d % n)


PLANE = sorted(
    [(a, b, c) for a in range(SIDE) for b in range(SIDE) for c in range(CORES)],
    key=lambda o: (-ring(o[0], SIDE) - ring(o[1], SIDE), -o[2]),
)
LINE = [o for o in PLANE if o[0] == 0]


def kernel(
    dims, snode, level, slots, f_hbm, low_hbm, up_hbm, piv_hbm, low_ref, up_ref,
    tbl, rlev, f_ref, low, up, piv, f2, held, land, psend, precv, xs, xrecv, last, zrecv,
    sem_in, send1, recv1, send2, recv2, send3, recv3, send4, recv4,
):
    rows, cols, nrow, nslot, ncol = dims
    nrhs = held.shape[1]
    per = rows // cols
    blocks = nrow * nslot
    total_blocks = rows * nrow
    zero = ROUNDS * ncol
    row, col = lax.axis_index("row"), lax.axis_index("col")
    y, x, core = row // (SIDE * CORES), row // CORES % SIDE, row % CORES
    base, lane = (row // cols) * cols, row % cols
    on_diag = col == lane
    off_diag = jnp.logical_not(on_diag)
    own_pos = row // cols + per * lane
    ys = [lax.rem(y + d, SIDE) * (SIDE * CORES) for d in range(SIDE)]
    xc = [[lax.rem(x + d, SIDE) * CORES + lax.rem(core + e, CORES) for e in range(CORES)] for d in range(SIDE)]
    zs = sorted(range(1, cols), key=lambda d: -ring(d, cols))

    copies = [
        pltpu.make_async_copy(src, dst, sem_in.at[k])
        for k, (src, dst) in enumerate([(low_hbm, low), (up_hbm, up), (f_hbm, f_ref), (piv_hbm, piv)])
    ]
    for copy in copies:
        copy.start()

    barrier = pltpu.get_barrier_semaphore()

    def greet(to):
        pl.semaphore_signal(barrier, inc=1, device_id=to, device_id_type=MESH)

    for dy, dx, dc in PLANE[:-1]:
        greet((ys[dy] + xc[dx][dc], col))
    for d in zs:
        greet((row, lax.rem(col + d, cols)))
    for _, dx, dc in LINE[:-1]:
        greet((base + xc[dx][dc], lane))
    for d in zs:
        greet((base + col, lax.rem(col + d, cols)))

    @pl.when(off_diag)
    def _():
        greet((base + lane, lane))
        greet((base + col, col))

    for i in range(nrow):
        rlev[i] = level[snode[row + rows * i]]

    own_level = level[snode[base + col + rows * lane]]

    def slot(b, carry):
        i = b // nslot
        this = row + rows * i
        lev, sn = rlev[i], snode[this]
        j = slots[b]
        valid = j < total_blocks
        jj = jnp.minimum(j, total_blocks - 1)
        j_sn = snode[jj]
        j_lev = level[j_sn]
        same = valid & (j_sn == sn)
        other = valid & (j_sn != sn)
        place = jj // cols
        lo_in = jnp.where((same & (j < this)) | (j == this), place, FAR)
        up_in = jnp.where((same & (j > this)) | (j == this), place, FAR)
        lo_out = jnp.where(other & (lev > j_lev), (2 * j_lev + 1) * ncol + place, zero)
        up_out = jnp.where(other & (lev < j_lev), (2 * (TOP - j_lev) + 1) * ncol + place, zero)
        for t in range(LEVELS):
            pick = jnp.where(lev == t, lo_in, jnp.where(lev == TOP - t, up_in, FAR))
            tbl[2 * t * blocks + b] = jnp.minimum(pick + 2 * t * ncol, zero)
            if t < TOP:
                pick = jnp.where(lev == t + 1, lo_out, jnp.where(lev == TOP - 1 - t, up_out, zero))
                tbl[(2 * t + 1) * blocks + b] = pick
        return carry

    lax.fori_loop(0, blocks, slot, 0)

    def one(flag):
        return jnp.where(flag, 1.0, 0.0).astype(jnp.float32)

    copies[0].wait()
    copies[1].wait()
    for j in range(ncol):
        lev = level[snode[j * cols + col]]
        rows_of = pl.ds(j, nrhs, stride=ncol)
        held[j] = (one(lev == 0) * low[rows_of, :] + one(lev == TOP) * up[rows_of, :]).astype(jnp.bfloat16)
    held[zero] = jnp.zeros(held.shape[1:], held.dtype)
    xs[...] = jnp.zeros_like(xs)
    mine_rows = pl.ds(own_pos, nrhs, stride=ncol)

    r_id = lax.broadcasted_iota(jnp.int32, f_ref.shape[1:], 0)
    c_id = lax.broadcasted_iota(jnp.int32, f_ref.shape[1:], 1)
    below = (c_id < r_id).astype(jnp.float32)
    above = (c_id > r_id).astype(jnp.float32)
    copies[2].wait()
    copies[3].wait()

    def mask_block(b, carry):
        block = f_ref[b].astype(jnp.float32)
        d = one(slots[b] == row + rows * (b // nslot))
        f2[b] = (block * (1.0 - d + d * below)).astype(jnp.bfloat16)
        f2[blocks + b] = (block * (1.0 - d + d * above)).astype(jnp.bfloat16)
        return carry

    lax.fori_loop(0, blocks, mask_block, 0)

    def row_sum(n, i, t):
        acc = None
        lev = rlev[i]
        sel = 0
        if t is not None:
            sel = jnp.where(lev == TOP - t, blocks, 0)
        for s in range(nslot):
            b = i * nslot + s
            term = lax.dot_general(
                held[tbl[n * blocks + b]], f2[sel + b], NT, preferred_element_type=jnp.float32
            )
            acc = term if acc is None else acc + term
        if t is not None:
            own = held[n * ncol + row // cols + per * i].astype(jnp.float32)
            w = one(on_diag & (lev == t)) + one(on_diag & (lev == TOP - t)) * piv[pl.ds(i, 1), :]
            acc = acc + w * own
        return acc

    def part_copy(n, i, dx, dc):
        return pltpu.make_async_remote_copy(
            src_ref=psend.at[n, i], dst_ref=precv.at[n, col], send_sem=send1.at[n], recv_sem=recv1.at[n],
            device_id=(base + i, lane), device_id_type=MESH,
        )

    def parts(n, t, wait_first):
        if wait_first:
            for _, dx, dc in LINE:
                i = xc[dx][dc]
                psend[n, i] = row_sum(n, i, t).astype(jnp.bfloat16)
            wait_first()
        for _, dx, dc in LINE:
            i = xc[dx][dc]
            if not wait_first:
                psend[n, i] = row_sum(n, i, t).astype(jnp.bfloat16)
            if dx or dc:
                part_copy(n, i, dx, dc).start()
            else:
                @pl.when(off_diag)
                def _():
                    part_copy(n, i, dx, dc).start()

                @pl.when(on_diag)
                def _():
                    precv[n, col] = psend[n, i]

    def wait_bytes(ref, count, sem):
        @pl.when(on_diag)
        def _():
            part = ref.at[pl.ds(0, count - 1)]
            pltpu.make_async_copy(part, part, sem).wait()

        @pl.when(off_diag)
        def _():
            part = ref.at[pl.ds(0, count)]
            pltpu.make_async_copy(part, part, sem).wait()

    def gathered(n):
        wait_bytes(precv.at[n], cols, recv1.at[n])
        return jnp.sum(precv[n].astype(jnp.float32), axis=0)

    def spread(n, value):
        land[n, own_pos] = value.astype(jnp.bfloat16)
        mine = land.at[n, own_pos]
        for dy, dx, dc in PLANE[:-1]:
            pltpu.make_async_remote_copy(
                src_ref=mine, dst_ref=mine, send_sem=send2.at[n], recv_sem=recv2.at[n],
                device_id=(ys[dy] + xc[dx][dc], col), device_id_type=MESH,
            ).start()

    def spread_wait(n):
        some = land.at[n, pl.ds(0, rows - 1)]
        pltpu.make_async_copy(some, some, recv2.at[n]).wait()
        held[pl.ds((n + 1) * ncol, ncol)] = land[n]

    def give_copy(d):
        return pltpu.make_async_remote_copy(
            src_ref=xs, dst_ref=xrecv.at[lane], send_sem=send3, recv_sem=recv3,
            device_id=(base + col, lax.rem(col + d, cols)), device_id_type=MESH,
        )

    def give():
        for d in zs:
            give_copy(d).start()

        @pl.when(off_diag)
        def _():
            give_copy(0).start()

        @pl.when(on_diag)
        def _():
            xrecv[lane] = xs[...]

    n_in = jnp.where(on_diag, 2 * (cols - 1), 2 * cols) + rows - 1 + cols - 1

    def level_step(t, first):
        n = 2 * t
        parts(n, t, first)
        sol = gathered(n)
        spread(n, sol)
        xs[0] += one(own_level == t) * sol
        xs[1] += one(own_level == TOP - t) * sol

        @pl.when(t == TOP - 1)
        def _():
            give()

        spread_wait(n)
        parts(n + 1, None, None)
        w = gathered(n + 1)
        rhs = one(own_level == t + 1) * low[mine_rows, :] + one(own_level == TOP - 1 - t) * up[mine_rows, :]
        spread(n + 1, rhs - w)
        spread_wait(n + 1)

    level_step(0, lambda: pl.semaphore_wait(barrier, n_in))

    def body(t, carry):
        level_step(t, None)
        return carry

    lax.fori_loop(1, TOP, body, 0)

    n = ROUNDS - 1
    for i in range(nrow):
        last[i] = row_sum(n, i, TOP).astype(jnp.bfloat16)
    zrecv[col] = last[...]
    for d in zs:
        pltpu.make_async_remote_copy(
            src_ref=last, dst_ref=zrecv.at[col], send_sem=send4, recv_sem=recv4,
            device_id=(row, lax.rem(col + d, cols)), device_id_type=MESH,
        ).start()

    def drain(m, carry):
        wait_bytes(psend.at[m], cols, send1.at[m])
        some = land.at[m, pl.ds(0, rows - 1)]
        pltpu.make_async_copy(some, some, send2.at[m]).wait()
        return carry

    lax.fori_loop(0, ROUNDS - 1, drain, 0)
    wait_bytes(xrecv, cols, recv3)
    wait_bytes(xrecv, cols, send3)
    some = zrecv.at[pl.ds(0, cols - 1)]
    pltpu.make_async_copy(some, some, recv4).wait()
    for i in range(nrow):
        sol = jnp.sum(zrecv[:, i].astype(jnp.float32), axis=0)
        lev = rlev[i]
        low_ref[:, i, :] = xrecv[i, 0] + one(lev == TOP) * sol
        up_ref[:, i, :] = xrecv[i, 1] + one(lev == 0) * sol
    pltpu.make_async_copy(some, some, send4).wait()


def shards(factor, inverse_pivot, lower_rhs, upper_rhs, snode_of_block, level_of_snode, slot_columns):
    rows, cols = lax.axis_size("row"), lax.axis_size("col")
    nrow, nslot, size = factor.shape[:3]
    nrhs, ncol = lower_rhs.shape[:2]
    f32, bf16 = jnp.float32, jnp.bfloat16
    blocks = nrow * nslot
    vmem, smem = pl.BlockSpec(memory_space=pltpu.VMEM), pl.BlockSpec(memory_space=pltpu.SMEM)
    hbm = pl.BlockSpec(memory_space=pl.ANY)
    dma = pltpu.SemaphoreType.DMA
    return pl.pallas_call(
        functools.partial(kernel, (rows, cols, nrow, nslot, ncol)),
        out_shape=[jax.ShapeDtypeStruct((nrhs, nrow, size), f32)] * 2,
        in_specs=[smem, smem, smem, hbm, hbm, hbm, hbm],
        out_specs=[vmem, vmem],
        scratch_shapes=[
            pltpu.SMEM((ROUNDS * blocks,), jnp.int32),
            pltpu.SMEM((nrow,), jnp.int32),
            pltpu.VMEM((blocks, size, size), bf16),
            pltpu.VMEM((nrhs * ncol, size), f32),
            pltpu.VMEM((nrhs * ncol, size), f32),
            pltpu.VMEM((nrow, size), f32),
            pltpu.VMEM((2 * blocks, size, size), bf16),
            pltpu.VMEM((ROUNDS * ncol + 1, nrhs, size), bf16),
            pltpu.VMEM((ROUNDS - 1, ncol, nrhs, size), bf16),
            pltpu.VMEM((ROUNDS - 1, nrow, nrhs, size), bf16),
            pltpu.VMEM((ROUNDS - 1, cols, nrhs, size), bf16),
            pltpu.VMEM((2, nrhs, size), f32),
            pltpu.VMEM((nrow, 2, nrhs, size), f32),
            pltpu.VMEM((nrow, nrhs, size), bf16),
            pltpu.VMEM((cols, nrow, nrhs, size), bf16),
            dma((4,)),
            dma((ROUNDS - 1,)), dma((ROUNDS - 1,)), dma((ROUNDS - 1,)), dma((ROUNDS - 1,)),
            dma, dma, dma, dma,
        ],
        compiler_params=pltpu.CompilerParams(
            collective_id=0, has_side_effects=True, vmem_limit_bytes=32 * 2**20
        ),
        cost_estimate=pl.CostEstimate(
            flops=2 * ROUNDS * blocks * size * size * nrhs,
            bytes_accessed=4 * blocks * size * size, transcendentals=0,
        ),
    )(
        snode_of_block, level_of_snode, slot_columns.reshape(-1),
        factor.reshape(blocks, size, size), lower_rhs.reshape(nrhs * ncol, size),
        upper_rhs.reshape(nrhs * ncol, size), inverse_pivot,
    )


def solution(mesh):
    in_specs = (
        P("row", "col", None, None),
        P("row", None),
        P(None, "col", None),
        P(None, "col", None),
        P(),
        P(),
        P("row", "col"),
    )
    out_specs = (P(None, "row", None), P(None, "row", None))
    return jax.shard_map(shards, mesh=mesh, in_specs=in_specs, out_specs=out_specs, check_vma=False)
```

```python
import functools

import jax
import jax.numpy as jnp
from jax import lax
from jax.experimental import pallas as pl
from jax.experimental.pallas import tpu as pltpu
from jax.sharding import PartitionSpec as P

MESH = pl.DeviceIdType.MESH
LEVELS = 6
TOP = LEVELS - 1
ROUNDS = 2 * LEVELS - 1
SIDE, CORES = 4, 2
FAR = 4096
VMEM_MIB = 60


def ring(d, n):
    return min(d % n, -d % n)


PLANE = sorted(
    [(a, b, c) for a in range(SIDE) for b in range(SIDE) for c in range(CORES)],
    key=lambda o: (-ring(o[0], SIDE) - ring(o[1], SIDE), -o[2]),
)
LINE = [o for o in PLANE if o[0] == 0]


def kernel(
    dims, snode, level, slots, f_hbm, low_hbm, up_hbm, piv_hbm, low_ref, up_ref,
    tbl, rlev, f_ref, low, up, piv, f2, piv8, own_piv, held, land, psend, precv, xs, xrecv, last, zrecv,
    sem_in, send1, recv1, send2, recv2, send3, recv3, send4, recv4, send5, recv5,
):
    rows, cols, nrow, nslot, ncol = dims
    nrhs = held.shape[1]
    per = rows // cols
    blocks = nrow * nslot
    total_blocks = rows * nrow
    zero = ROUNDS * ncol
    row, col = lax.axis_index("row"), lax.axis_index("col")
    y, x, core = row // (SIDE * CORES), row // CORES % SIDE, row % CORES
    base, lane = (row // cols) * cols, row % cols
    on_diag = col == lane
    off_diag = jnp.logical_not(on_diag)
    own_pos = row // cols + per * lane
    ys = [lax.rem(y + d, SIDE) * (SIDE * CORES) for d in range(SIDE)]
    xc = [[lax.rem(x + d, SIDE) * CORES + lax.rem(core + e, CORES) for e in range(CORES)] for d in range(SIDE)]
    zs = sorted(range(1, cols), key=lambda d: -ring(d, cols))

    copies = [
        pltpu.make_async_copy(src, dst, sem_in.at[k])
        for k, (src, dst) in enumerate([(f_hbm, f_ref), (low_hbm, low), (up_hbm, up), (piv_hbm, piv)])
    ]
    for copy in copies:
        copy.start()

    barrier = pltpu.get_barrier_semaphore()

    def greet(to):
        pl.semaphore_signal(barrier, inc=1, device_id=to, device_id_type=MESH)

    for d in zs:
        greet((base + col, lax.rem(col + d, cols)))
    for _, dx, dc in LINE[:-1]:
        greet((base + xc[dx][dc], lane))

    @pl.when(off_diag)
    def _():
        greet((base + lane, lane))
        greet((base + col, col))

    for dy, dx, dc in PLANE[:-1]:
        greet((ys[dy] + xc[dx][dc], col))
    for d in zs:
        greet((row, lax.rem(col + d, cols)))

    for i in range(nrow):
        rlev[i] = level[snode[row + rows * i]]

    own_level = level[snode[base + col + rows * lane]]

    def slot(b, carry):
        i = b // nslot
        this = row + rows * i
        lev, sn = rlev[i], snode[this]
        j = slots[b % nslot, i]
        valid = j < total_blocks
        jj = jnp.minimum(j, total_blocks - 1)
        j_sn = snode[jj]
        j_lev = level[j_sn]
        same = valid & (j_sn == sn)
        other = valid & (j_sn != sn)
        place = jj // cols
        lo_in = jnp.where((same & (j < this)) | (j == this), place, FAR)
        up_in = jnp.where((same & (j > this)) | (j == this), place, FAR)
        lo_out = jnp.where(other & (lev > j_lev), (2 * j_lev + 1) * ncol + place, zero)
        up_out = jnp.where(other & (lev < j_lev), (2 * (TOP - j_lev) + 1) * ncol + place, zero)
        for t in range(LEVELS):
            pick = jnp.where(lev == t, lo_in, jnp.where(lev == TOP - t, up_in, FAR))
            tbl[2 * t * blocks + b] = jnp.minimum(pick + 2 * t * ncol, zero)
            if t < TOP:
                pick = jnp.where(lev == t + 1, lo_out, jnp.where(lev == TOP - 1 - t, up_out, zero))
                tbl[(2 * t + 1) * blocks + b] = pick
        return carry

    lax.fori_loop(0, blocks, slot, 0)

    def one(flag):
        return jnp.where(flag, 1.0, 0.0).astype(jnp.float32)

    copies[1].wait()
    copies[2].wait()
    for j in range(ncol):
        lev = level[snode[j * cols + col]]
        rows_of = pl.ds(j, nrhs, stride=ncol)
        held[j] = (one(lev == 0) * low[rows_of, :] + one(lev == TOP) * up[rows_of, :]).astype(jnp.bfloat16)
    held[zero] = jnp.zeros(held.shape[1:], held.dtype)
    xs[...] = jnp.zeros_like(xs)
    mine_rows = pl.ds(own_pos, nrhs, stride=ncol)

    r_id = lax.broadcasted_iota(jnp.int32, f_ref.shape[1:], 0)
    c_id = lax.broadcasted_iota(jnp.int32, f_ref.shape[1:], 1)
    below = jnp.where(r_id < c_id, 0.0, -1.0).astype(jnp.bfloat16)
    above = jnp.where(r_id > c_id, 0.0, -1.0).astype(jnp.bfloat16)
    copies[0].wait()
    copies[3].wait()
    for i in range(nrow):
        piv8[i] = jnp.broadcast_to(piv[i : i + 1, :], piv8.shape[1:])

    def mask_block(b, carry):
        block = f_ref[b].T
        d = one(slots[b % nslot, b // nslot] == row + rows * (b // nslot)).astype(jnp.bfloat16)
        i, at = b // nslot, pl.ds(pl.multiple_of(b % nslot * f_ref.shape[1], f_ref.shape[1]), f_ref.shape[1])
        f2[i, at] = block + block * (d * below)
        f2[nrow + i, at] = block + block * (d * above)
        return carry

    lax.fori_loop(0, blocks, mask_block, 0, unroll=4)

    def row_sum(n, i, t):
        side = i if t is None else i + jnp.where(rlev[i] == TOP - t, nrow, 0)
        picked = [held[tbl[n * blocks + i * nslot + s]] for s in range(nslot)]
        return jnp.dot(jnp.concatenate(picked, axis=1), f2[side], preferred_element_type=jnp.float32)

    def part_copy(n, i):
        return pltpu.make_async_remote_copy(
            src_ref=psend.at[n, i], dst_ref=precv.at[n, col], send_sem=send1.at[n], recv_sem=recv1.at[n],
            device_id=(base + i, lane), device_id_type=MESH,
        )

    def parts(n, t, ready):
        sums = [row_sum(n, xc[dx][dc], t) for _, dx, dc in LINE]
        for (_, dx, dc), value in zip(LINE, sums):
            psend[n, xc[dx][dc]] = value.astype(jnp.bfloat16)
        ready()
        for _, dx, dc in LINE[:-1]:
            part_copy(n, xc[dx][dc]).start()

        @pl.when(off_diag)
        def _():
            part_copy(n, lane).start()

        @pl.when(on_diag)
        def _():
            precv[n, col] = psend[n, col]

    def wait_bytes(ref, count, sem):
        @pl.when(on_diag)
        def _():
            part = ref.at[pl.ds(0, count - 1)]
            pltpu.make_async_copy(part, part, sem).wait()

        @pl.when(off_diag)
        def _():
            part = ref.at[pl.ds(0, count)]
            pltpu.make_async_copy(part, part, sem).wait()

    def gathered(n):
        wait_bytes(precv.at[n], cols, recv1.at[n])
        return jnp.sum(precv[n].astype(jnp.float32), axis=0)

    def spread(n, value):
        land[n, own_pos] = value.astype(jnp.bfloat16)
        mine = land.at[n, own_pos]
        for dy, dx, dc in PLANE[:-1]:
            pltpu.make_async_remote_copy(
                src_ref=mine, dst_ref=mine, send_sem=send2.at[n], recv_sem=recv2.at[n],
                device_id=(ys[dy] + xc[dx][dc], col), device_id_type=MESH,
            ).start()

    def spread_wait(n):
        some = land.at[n, pl.ds(0, rows - 1)]
        pltpu.make_async_copy(some, some, recv2.at[n]).wait()
        held[pl.ds((n + 1) * ncol, ncol)] = land[n]

    def give_copy(d):
        return pltpu.make_async_remote_copy(
            src_ref=xs, dst_ref=xrecv.at[lane], send_sem=send3, recv_sem=recv3,
            device_id=(base + col, lax.rem(col + d, cols)), device_id_type=MESH,
        )

    def give():
        for d in zs:
            give_copy(d).start()

        @pl.when(off_diag)
        def _():
            give_copy(0).start()

        @pl.when(on_diag)
        def _():
            xrecv[lane] = xs[...]

    def piv_copy(to, i):
        return pltpu.make_async_remote_copy(
            src_ref=piv8.at[i], dst_ref=own_piv, send_sem=send5, recv_sem=recv5,
            device_id=(base + to, lane), device_id_type=MESH,
        )

    def pivots_start():
        @pl.when(on_diag)
        def _():
            for _, dx, dc in LINE[:-1]:
                piv_copy(xc[dx][dc], xc[dx][dc]).start()
            own_piv[...] = piv8[lane]

    def pivots_wait():
        @pl.when(on_diag)
        def _():
            some = piv8.at[pl.ds(0, cols - 1)]
            pltpu.make_async_copy(some, some, send5).wait()

        @pl.when(off_diag)
        def _():
            pltpu.make_async_copy(own_piv, own_piv, recv5).wait()

    n_in = jnp.where(on_diag, 2 * (cols - 1), 2 * cols) + rows - 1 + cols - 1

    def level_step(t, first):
        n = 2 * t
        parts(n, t, lambda: pl.semaphore_wait(barrier, n_in) if first else None)
        if first:
            pivots_start()
        sol = gathered(n)
        if first:
            pivots_wait()
        own = held[n * ncol + own_pos].astype(jnp.float32)
        sol = sol + (one(own_level == t) + one(own_level == TOP - t) * own_piv[0:1, :]) * own
        spread(n, sol)
        xs[0] += one(own_level == t) * sol
        xs[1] += one(own_level == TOP - t) * sol

        @pl.when(t == TOP - 1)
        def _():
            give()

        spread_wait(n)
        parts(n + 1, None, lambda: None)
        w = gathered(n + 1)
        rhs = one(own_level == t + 1) * low[mine_rows, :] + one(own_level == TOP - 1 - t) * up[mine_rows, :]
        spread(n + 1, rhs - w)
        spread_wait(n + 1)

    level_step(0, True)

    def body(t, carry):
        level_step(t, False)
        return carry

    lax.fori_loop(1, TOP, body, 0)

    n = ROUNDS - 1
    for i in range(nrow):
        own = held[n * ncol + row // cols + per * i].astype(jnp.float32)
        w = one(on_diag & (rlev[i] == TOP)) + one(on_diag & (rlev[i] == 0)) * piv8[i, 0:1, :]
        last[i] = (row_sum(n, i, TOP) + w * own).astype(jnp.bfloat16)
    zrecv[col] = last[...]
    for d in zs:
        pltpu.make_async_remote_copy(
            src_ref=last, dst_ref=zrecv.at[col], send_sem=send4, recv_sem=recv4,
            device_id=(row, lax.rem(col + d, cols)), device_id_type=MESH,
        ).start()

    def drain(m, carry):
        wait_bytes(psend.at[m], cols, send1.at[m])
        some = land.at[m, pl.ds(0, rows - 1)]
        pltpu.make_async_copy(some, some, send2.at[m]).wait()
        return carry

    lax.fori_loop(0, ROUNDS - 1, drain, 0)
    wait_bytes(xrecv, cols, recv3)
    wait_bytes(xrecv, cols, send3)
    some = zrecv.at[pl.ds(0, cols - 1)]
    pltpu.make_async_copy(some, some, recv4).wait()
    for i in range(nrow):
        sol = jnp.sum(zrecv[:, i].astype(jnp.float32), axis=0)
        lev = rlev[i]
        low_ref[:, i, :] = xrecv[i, 0] + one(lev == TOP) * sol
        up_ref[:, i, :] = xrecv[i, 1] + one(lev == 0) * sol
    pltpu.make_async_copy(some, some, send4).wait()


def shards(factor, inverse_pivot, lower_rhs, upper_rhs, snode_of_block, level_of_snode, slot_columns):
    rows, cols = lax.axis_size("row"), lax.axis_size("col")
    nrow, nslot, size = factor.shape[:3]
    nrhs, ncol = lower_rhs.shape[:2]
    f32, bf16 = jnp.float32, jnp.bfloat16
    blocks = nrow * nslot
    vmem, smem = pl.BlockSpec(memory_space=pltpu.VMEM), pl.BlockSpec(memory_space=pltpu.SMEM)
    hbm = pl.BlockSpec(memory_space=pltpu.HBM)
    dma = pltpu.SemaphoreType.DMA
    return pl.pallas_call(
        functools.partial(kernel, (rows, cols, nrow, nslot, ncol)),
        out_shape=[jax.ShapeDtypeStruct((nrhs, nrow, size), f32)] * 2,
        in_specs=[smem, smem, smem, hbm, hbm, hbm, hbm],
        out_specs=[vmem, vmem],
        scratch_shapes=[
            pltpu.SMEM((ROUNDS * blocks,), jnp.int32),
            pltpu.SMEM((nrow,), jnp.int32),
            pltpu.VMEM((blocks, size, size), bf16),
            pltpu.VMEM((nrhs * ncol, size), f32),
            pltpu.VMEM((nrhs * ncol, size), f32),
            pltpu.VMEM((nrow, size), f32),
            pltpu.VMEM((2 * nrow, nslot * size, size), bf16),
            pltpu.VMEM((nrow, 8, size), f32),
            pltpu.VMEM((8, size), f32),
            pltpu.VMEM((ROUNDS * ncol + 1, nrhs, size), bf16),
            pltpu.VMEM((ROUNDS - 1, ncol, nrhs, size), bf16),
            pltpu.VMEM((ROUNDS - 1, nrow, nrhs, size), bf16),
            pltpu.VMEM((ROUNDS - 1, cols, nrhs, size), bf16),
            pltpu.VMEM((2, nrhs, size), f32),
            pltpu.VMEM((nrow, 2, nrhs, size), f32),
            pltpu.VMEM((nrow, nrhs, size), bf16),
            pltpu.VMEM((cols, nrow, nrhs, size), bf16),
            dma((4,)),
            dma((ROUNDS - 1,)), dma((ROUNDS - 1,)), dma((ROUNDS - 1,)), dma((ROUNDS - 1,)),
            dma, dma, dma, dma, dma, dma,
        ],
        compiler_params=pltpu.CompilerParams(
            collective_id=0, has_side_effects=True, vmem_limit_bytes=VMEM_MIB * 2**20
        ),
        cost_estimate=pl.CostEstimate(
            flops=2 * ROUNDS * blocks * size * size * nrhs,
            bytes_accessed=4 * blocks * size * size, transcendentals=0,
        ),
    )(
        snode_of_block, level_of_snode, slot_columns.T,
        factor.reshape(blocks, size, size), lower_rhs.reshape(nrhs * ncol, size),
        upper_rhs.reshape(nrhs * ncol, size), inverse_pivot,
    )


def solution(mesh):
    in_specs = (
        P("row", "col", None, None),
        P("row", None),
        P(None, "col", None),
        P(None, "col", None),
        P(),
        P(),
        P("row", "col"),
    )
    out_specs = (P(None, "row", None), P(None, "row", None))
    return jax.shard_map(shards, mesh=mesh, in_specs=in_specs, out_specs=out_specs, check_vma=False)
```

```python
import functools

import jax
import jax.numpy as jnp
from jax import lax
from jax.experimental import pallas as pl
from jax.experimental.pallas import tpu as pltpu
from jax.sharding import PartitionSpec as P

MESH = pl.DeviceIdType.MESH
LEVELS = 6
TOP = LEVELS - 1
ROUNDS = 2 * LEVELS - 1
SIDE, CORES = 4, 2
FAR = 4096
VMEM_MIB = 53.75


def ring(d, n):
    return min(d % n, -d % n)


PLANE = sorted(
    [(a, b, c) for a in range(SIDE) for b in range(SIDE) for c in range(CORES)],
    key=lambda o: (-ring(o[0], SIDE) - ring(o[1], SIDE), -o[2]),
)
LINE = [o for o in PLANE if o[0] == 0]


def kernel(
    dims, snode_hbm, level_hbm, slots_hbm, f_hbm, low_hbm, up_hbm, piv_hbm, low_ref, up_ref,
    snode, level, slots, tbl, rlev, f_ref, low, up, piv, f2, piv8, own_piv, held, land, psend, precv, xs, xrecv, last, zrecv,
    sem_in, send1, recv1, send2, recv2, send3, recv3, send4, recv4, send5, recv5,
):
    rows, cols, nrow, nslot, ncol = dims
    nrhs = held.shape[1]
    per = rows // cols
    blocks = nrow * nslot
    total_blocks = rows * nrow
    zero = ROUNDS * ncol
    row, col = lax.axis_index("row"), lax.axis_index("col")
    y, x, core = row // (SIDE * CORES), row // CORES % SIDE, row % CORES
    base, lane = (row // cols) * cols, row % cols
    on_diag = col == lane
    off_diag = jnp.logical_not(on_diag)
    own_pos = row // cols + per * lane
    ys = [lax.rem(y + d, SIDE) * (SIDE * CORES) for d in range(SIDE)]
    xc = [[lax.rem(x + d, SIDE) * CORES + lax.rem(core + e, CORES) for e in range(CORES)] for d in range(SIDE)]
    zs = sorted(range(1, cols), key=lambda d: -ring(d, cols))

    copies = [
        pltpu.make_async_copy(src, dst, sem_in.at[k])
        for k, (src, dst) in enumerate([(f_hbm, f_ref), (low_hbm, low), (up_hbm, up), (piv_hbm, piv),
            (snode_hbm, snode), (level_hbm, level), (slots_hbm, slots)])
    ]
    for copy in copies:
        copy.start()

    barrier = pltpu.get_barrier_semaphore()

    def greet(to):
        pl.semaphore_signal(barrier, inc=1, device_id=to, device_id_type=MESH)

    for d in zs:
        greet((base + col, lax.rem(col + d, cols)))
    for _, dx, dc in LINE[:-1]:
        greet((base + xc[dx][dc], lane))

    @pl.when(off_diag)
    def _():
        greet((base + lane, lane))
        greet((base + col, col))

    for dy, dx, dc in PLANE[:-1]:
        greet((ys[dy] + xc[dx][dc], col))
    for d in zs:
        greet((row, lax.rem(col + d, cols)))

    for copy in copies[4:]:
        copy.wait()
    for i in range(nrow):
        rlev[i] = level[snode[row + rows * i]]

    own_level = level[snode[base + col + rows * lane]]

    def slot(b, carry):
        i = b // nslot
        this = row + rows * i
        lev, sn = rlev[i], snode[this]
        j = slots[b % nslot, i]
        valid = j < total_blocks
        jj = jnp.minimum(j, total_blocks - 1)
        j_sn = snode[jj]
        j_lev = level[j_sn]
        same = valid & (j_sn == sn)
        other = valid & (j_sn != sn)
        place = jj // cols
        lo_in = jnp.where((same & (j < this)) | (j == this), place, FAR)
        up_in = jnp.where((same & (j > this)) | (j == this), place, FAR)
        lo_out = jnp.where(other & (lev > j_lev), (2 * j_lev + 1) * ncol + place, zero)
        up_out = jnp.where(other & (lev < j_lev), (2 * (TOP - j_lev) + 1) * ncol + place, zero)
        for t in range(LEVELS):
            pick = jnp.where(lev == t, lo_in, jnp.where(lev == TOP - t, up_in, FAR))
            tbl[2 * t * blocks + b] = jnp.minimum(pick + 2 * t * ncol, zero)
            if t < TOP:
                pick = jnp.where(lev == t + 1, lo_out, jnp.where(lev == TOP - 1 - t, up_out, zero))
                tbl[(2 * t + 1) * blocks + b] = pick
        return carry

    lax.fori_loop(0, blocks, slot, 0)

    def one(flag):
        return jnp.where(flag, 1.0, 0.0).astype(jnp.float32)

    copies[1].wait()
    copies[2].wait()
    for j in range(ncol):
        lev = level[snode[j * cols + col]]
        rows_of = pl.ds(j, nrhs, stride=ncol)
        held[j] = (one(lev == 0) * low[rows_of, :] + one(lev == TOP) * up[rows_of, :]).astype(jnp.bfloat16)
    held[zero] = jnp.zeros(held.shape[1:], held.dtype)
    xs[...] = jnp.zeros_like(xs)
    mine_rows = pl.ds(own_pos, nrhs, stride=ncol)

    r_id = lax.broadcasted_iota(jnp.int32, f_ref.shape[1:], 0)
    c_id = lax.broadcasted_iota(jnp.int32, f_ref.shape[1:], 1)
    below = jnp.where(r_id < c_id, 0.0, -1.0).astype(jnp.bfloat16)
    above = jnp.where(r_id > c_id, 0.0, -1.0).astype(jnp.bfloat16)
    copies[0].wait()
    copies[3].wait()
    for i in range(nrow):
        piv8[i] = jnp.broadcast_to(piv[i : i + 1, :], piv8.shape[1:])

    def mask_block(b, carry):
        block = f_ref[b].T
        d = one(slots[b % nslot, b // nslot] == row + rows * (b // nslot)).astype(jnp.bfloat16)
        i, at = b // nslot, pl.ds(pl.multiple_of(b % nslot * f_ref.shape[1], f_ref.shape[1]), f_ref.shape[1])
        f2[i, at] = block + block * (d * below)
        f2[nrow + i, at] = block + block * (d * above)
        return carry

    lax.fori_loop(0, blocks, mask_block, 0, unroll=4)

    def row_sum(n, i, t):
        side = i if t is None else i + jnp.where(rlev[i] == TOP - t, nrow, 0)
        picked = [held[tbl[n * blocks + i * nslot + s]] for s in range(nslot)]
        return jnp.dot(jnp.concatenate(picked, axis=1), f2[side], preferred_element_type=jnp.float32)

    def part_copy(n, i):
        return pltpu.make_async_remote_copy(
            src_ref=psend.at[n, i], dst_ref=precv.at[n, col], send_sem=send1.at[n], recv_sem=recv1.at[n],
            device_id=(base + i, lane), device_id_type=MESH,
        )

    def parts(n, t, ready):
        sums = [row_sum(n, xc[dx][dc], t) for _, dx, dc in LINE]
        for (_, dx, dc), value in zip(LINE, sums):
            psend[n, xc[dx][dc]] = value.astype(jnp.bfloat16)
        ready()
        for _, dx, dc in LINE[:-1]:
            part_copy(n, xc[dx][dc]).start()

        @pl.when(off_diag)
        def _():
            part_copy(n, lane).start()

        @pl.when(on_diag)
        def _():
            precv[n, col] = psend[n, col]

    def wait_bytes(ref, count, sem):
        @pl.when(on_diag)
        def _():
            part = ref.at[pl.ds(0, count - 1)]
            pltpu.make_async_copy(part, part, sem).wait()

        @pl.when(off_diag)
        def _():
            part = ref.at[pl.ds(0, count)]
            pltpu.make_async_copy(part, part, sem).wait()

    def gathered(n):
        wait_bytes(precv.at[n], cols, recv1.at[n])
        return jnp.sum(precv[n].astype(jnp.float32), axis=0)

    def spread(n, value):
        land[n, own_pos] = value.astype(jnp.bfloat16)
        mine = land.at[n, own_pos]
        for dy, dx, dc in PLANE[:-1]:
            pltpu.make_async_remote_copy(
                src_ref=mine, dst_ref=mine, send_sem=send2.at[n], recv_sem=recv2.at[n],
                device_id=(ys[dy] + xc[dx][dc], col), device_id_type=MESH,
            ).start()

    def spread_wait(n):
        some = land.at[n, pl.ds(0, rows - 1)]
        pltpu.make_async_copy(some, some, recv2.at[n]).wait()
        held[pl.ds((n + 1) * ncol, ncol)] = land[n]

    def give_copy(d):
        return pltpu.make_async_remote_copy(
            src_ref=xs, dst_ref=xrecv.at[lane], send_sem=send3, recv_sem=recv3,
            device_id=(base + col, lax.rem(col + d, cols)), device_id_type=MESH,
        )

    def give():
        for d in zs:
            give_copy(d).start()

        @pl.when(off_diag)
        def _():
            give_copy(0).start()

        @pl.when(on_diag)
        def _():
            xrecv[lane] = xs[...]

    def piv_copy(to, i):
        return pltpu.make_async_remote_copy(
            src_ref=piv8.at[i], dst_ref=own_piv, send_sem=send5, recv_sem=recv5,
            device_id=(base + to, lane), device_id_type=MESH,
        )

    def pivots_start():
        @pl.when(on_diag)
        def _():
            for _, dx, dc in LINE[:-1]:
                piv_copy(xc[dx][dc], xc[dx][dc]).start()
            own_piv[...] = piv8[lane]

    def pivots_wait():
        @pl.when(on_diag)
        def _():
            some = piv8.at[pl.ds(0, cols - 1)]
            pltpu.make_async_copy(some, some, send5).wait()

        @pl.when(off_diag)
        def _():
            pltpu.make_async_copy(own_piv, own_piv, recv5).wait()

    n_in = jnp.where(on_diag, 2 * (cols - 1), 2 * cols) + rows - 1 + cols - 1

    def level_step(t, first):
        n = 2 * t
        parts(n, t, lambda: pl.semaphore_wait(barrier, n_in) if first else None)
        if first:
            pivots_start()
        sol = gathered(n)
        if first:
            pivots_wait()
        own = held[n * ncol + own_pos].astype(jnp.float32)
        sol = sol + (one(own_level == t) + one(own_level == TOP - t) * own_piv[0:1, :]) * own
        spread(n, sol)
        xs[0] += one(own_level == t) * sol
        xs[1] += one(own_level == TOP - t) * sol

        @pl.when(t == TOP - 1)
        def _():
            give()

        spread_wait(n)
        parts(n + 1, None, lambda: None)
        w = gathered(n + 1)
        rhs = one(own_level == t + 1) * low[mine_rows, :] + one(own_level == TOP - 1 - t) * up[mine_rows, :]
        spread(n + 1, rhs - w)
        spread_wait(n + 1)

    level_step(0, True)

    def body(t, carry):
        level_step(t, False)
        return carry

    lax.fori_loop(1, TOP, body, 0)

    n = ROUNDS - 1
    for i in range(nrow):
        own = held[n * ncol + row // cols + per * i].astype(jnp.float32)
        w = one(on_diag & (rlev[i] == TOP)) + one(on_diag & (rlev[i] == 0)) * piv8[i, 0:1, :]
        last[i] = (row_sum(n, i, TOP) + w * own).astype(jnp.bfloat16)
    zrecv[col] = last[...]
    for d in zs:
        pltpu.make_async_remote_copy(
            src_ref=last, dst_ref=zrecv.at[col], send_sem=send4, recv_sem=recv4,
            device_id=(row, lax.rem(col + d, cols)), device_id_type=MESH,
        ).start()

    def drain(m, carry):
        wait_bytes(psend.at[m], cols, send1.at[m])
        some = land.at[m, pl.ds(0, rows - 1)]
        pltpu.make_async_copy(some, some, send2.at[m]).wait()
        return carry

    lax.fori_loop(0, ROUNDS - 1, drain, 0)
    wait_bytes(xrecv, cols, recv3)
    wait_bytes(xrecv, cols, send3)
    some = zrecv.at[pl.ds(0, cols - 1)]
    pltpu.make_async_copy(some, some, recv4).wait()
    for i in range(nrow):
        sol = jnp.sum(zrecv[:, i].astype(jnp.float32), axis=0)
        lev = rlev[i]
        low_ref[:, i, :] = xrecv[i, 0] + one(lev == TOP) * sol
        up_ref[:, i, :] = xrecv[i, 1] + one(lev == 0) * sol
    pltpu.make_async_copy(some, some, send4).wait()


def shards(factor, inverse_pivot, lower_rhs, upper_rhs, snode_of_block, level_of_snode, slot_columns):
    rows, cols = lax.axis_size("row"), lax.axis_size("col")
    nrow, nslot, size = factor.shape[:3]
    nrhs, ncol = lower_rhs.shape[:2]
    f32, bf16 = jnp.float32, jnp.bfloat16
    blocks = nrow * nslot
    vmem = pl.BlockSpec(memory_space=pltpu.VMEM)
    hbm = pl.BlockSpec(memory_space=pltpu.HBM)
    dma = pltpu.SemaphoreType.DMA
    return pl.pallas_call(
        functools.partial(kernel, (rows, cols, nrow, nslot, ncol)),
        out_shape=[jax.ShapeDtypeStruct((nrhs, nrow, size), f32)] * 2,
        in_specs=[hbm] * 7,
        out_specs=[vmem, vmem],
        scratch_shapes=[
            pltpu.SMEM(snode_of_block.shape, jnp.int32),
            pltpu.SMEM(level_of_snode.shape, jnp.int32),
            pltpu.SMEM((nslot, nrow), jnp.int32),
            pltpu.SMEM((ROUNDS * blocks,), jnp.int32),
            pltpu.SMEM((nrow,), jnp.int32),
            pltpu.VMEM((blocks, size, size), bf16),
            pltpu.VMEM((nrhs * ncol, size), f32),
            pltpu.VMEM((nrhs * ncol, size), f32),
            pltpu.VMEM((nrow, size), f32),
            pltpu.VMEM((2 * nrow, nslot * size, size), bf16),
            pltpu.VMEM((nrow, 8, size), f32),
            pltpu.VMEM((8, size), f32),
            pltpu.VMEM((ROUNDS * ncol + 1, nrhs, size), bf16),
            pltpu.VMEM((ROUNDS - 1, ncol, nrhs, size), bf16),
            pltpu.VMEM((ROUNDS - 1, nrow, nrhs, size), bf16),
            pltpu.VMEM((ROUNDS - 1, cols, nrhs, size), bf16),
            pltpu.VMEM((2, nrhs, size), f32),
            pltpu.VMEM((nrow, 2, nrhs, size), f32),
            pltpu.VMEM((nrow, nrhs, size), bf16),
            pltpu.VMEM((cols, nrow, nrhs, size), bf16),
            dma((7,)),
            dma((ROUNDS - 1,)), dma((ROUNDS - 1,)), dma((ROUNDS - 1,)), dma((ROUNDS - 1,)),
            dma, dma, dma, dma, dma, dma,
        ],
        compiler_params=pltpu.CompilerParams(
            collective_id=0, has_side_effects=True, vmem_limit_bytes=int(VMEM_MIB * 2**20)
        ),
        cost_estimate=pl.CostEstimate(
            flops=2 * ROUNDS * blocks * size * size * nrhs,
            bytes_accessed=4 * blocks * size * size, transcendentals=0,
        ),
    )(
        snode_of_block, level_of_snode, slot_columns.T,
        factor.reshape(blocks, size, size), lower_rhs.reshape(nrhs * ncol, size),
        upper_rhs.reshape(nrhs * ncol, size), inverse_pivot,
    )


def solution(mesh):
    in_specs = (
        P("row", "col", None, None),
        P("row", None),
        P(None, "col", None),
        P(None, "col", None),
        P(),
        P(),
        P("row", "col"),
    )
    out_specs = (P(None, "row", None), P(None, "row", None))
    return jax.shard_map(shards, mesh=mesh, in_specs=in_specs, out_specs=out_specs, check_vma=False)
```

```python
import functools

import jax
import jax.numpy as jnp
from jax import lax
from jax.experimental import pallas as pl
from jax.experimental.pallas import tpu as pltpu
from jax.sharding import PartitionSpec as P

MESH = pl.DeviceIdType.MESH
LEVELS = 6
TOP = LEVELS - 1
ROUNDS = 2 * LEVELS - 1
SIDE, CORES = 4, 2
FAR = 4096
VMEM_BYTES = 32 * 2**20


def ring(d, n):
    return min(d % n, -d % n)


PLANE = sorted(
    [(a, b, c) for a in range(SIDE) for b in range(SIDE) for c in range(CORES)],
    key=lambda o: (-ring(o[0], SIDE) - ring(o[1], SIDE), -o[2]),
)
LINE = [o for o in PLANE if o[0] == 0]


def kernel(
    dims, snode_hbm, level_hbm, slots_hbm, f_hbm, low_hbm, up_hbm, piv_hbm, low_ref, up_ref,
    snode, level, slots, tbl, rlev, f_ref, low, up, piv, f2, piv8, own_piv, held, land, psend, precv, xs, xrecv, last, zrecv,
    sem_in, send1, recv1, send2, recv2, send3, recv3, send4, recv4, send5, recv5,
):
    rows, cols, nrow, nslot, ncol = dims
    nrhs = held.shape[1]
    per = rows // cols
    blocks = nrow * nslot
    total_blocks = rows * nrow
    zero = ROUNDS * ncol
    row, col = lax.axis_index("row"), lax.axis_index("col")
    y, x, core = row // (SIDE * CORES), row // CORES % SIDE, row % CORES
    base, lane = (row // cols) * cols, row % cols
    on_diag = col == lane
    off_diag = jnp.logical_not(on_diag)
    own_pos = row // cols + per * lane
    ys = [lax.rem(y + d, SIDE) * (SIDE * CORES) for d in range(SIDE)]
    xc = [[lax.rem(x + d, SIDE) * CORES + lax.rem(core + e, CORES) for e in range(CORES)] for d in range(SIDE)]
    zs = sorted(range(1, cols), key=lambda d: -ring(d, cols))

    barrier = pltpu.get_barrier_semaphore()

    def greet(to):
        pl.semaphore_signal(barrier, inc=1, device_id=to, device_id_type=MESH)

    for d in zs:
        greet((base + col, lax.rem(col + d, cols)))
    for _, dx, dc in LINE[:-1]:
        greet((base + xc[dx][dc], lane))

    @pl.when(off_diag)
    def _():
        greet((base + lane, lane))
        greet((base + col, col))

    copies = [
        pltpu.make_async_copy(src, dst, sem_in.at[k])
        for k, (src, dst) in enumerate([(f_hbm, f_ref), (low_hbm, low), (up_hbm, up), (piv_hbm, piv),
            (snode_hbm, snode), (level_hbm, level), (slots_hbm, slots)])
    ]
    for copy in copies:
        copy.start()

    for dy, dx, dc in PLANE[:-1]:
        greet((ys[dy] + xc[dx][dc], col))
    for d in zs:
        greet((row, lax.rem(col + d, cols)))

    for copy in copies[4:]:
        copy.wait()
    for i in range(nrow):
        rlev[i] = level[snode[row + rows * i]]

    own_level = level[snode[base + col + rows * lane]]

    def slot(b, carry):
        i = b // nslot
        this = row + rows * i
        lev, sn = rlev[i], snode[this]
        j = slots[b % nslot, i]
        valid = j < total_blocks
        jj = jnp.minimum(j, total_blocks - 1)
        j_sn = snode[jj]
        j_lev = level[j_sn]
        same = valid & (j_sn == sn)
        other = valid & (j_sn != sn)
        place = jj // cols
        lo_in = jnp.where((same & (j < this)) | (j == this), place, FAR)
        up_in = jnp.where((same & (j > this)) | (j == this), place, FAR)
        lo_out = jnp.where(other & (lev > j_lev), (2 * j_lev + 1) * ncol + place, zero)
        up_out = jnp.where(other & (lev < j_lev), (2 * (TOP - j_lev) + 1) * ncol + place, zero)
        for t in range(LEVELS):
            pick = jnp.where(lev == t, lo_in, jnp.where(lev == TOP - t, up_in, FAR))
            tbl[2 * t * blocks + b] = jnp.minimum(pick + 2 * t * ncol, zero)
            if t < TOP:
                pick = jnp.where(lev == t + 1, lo_out, jnp.where(lev == TOP - 1 - t, up_out, zero))
                tbl[(2 * t + 1) * blocks + b] = pick
        return carry

    lax.fori_loop(0, blocks, slot, 0)

    def one(flag):
        return jnp.where(flag, 1.0, 0.0).astype(jnp.float32)

    copies[1].wait()
    copies[2].wait()
    for j in range(ncol):
        lev = level[snode[j * cols + col]]
        rows_of = pl.ds(j, nrhs, stride=ncol)
        held[j] = (one(lev == 0) * low[rows_of, :] + one(lev == TOP) * up[rows_of, :]).astype(jnp.bfloat16)
    held[zero] = jnp.zeros(held.shape[1:], held.dtype)
    xs[...] = jnp.zeros_like(xs)
    mine_rows = pl.ds(own_pos, nrhs, stride=ncol)

    r_id = lax.broadcasted_iota(jnp.int32, f_ref.shape[1:], 0)
    c_id = lax.broadcasted_iota(jnp.int32, f_ref.shape[1:], 1)
    below = jnp.where(r_id < c_id, 0.0, -1.0).astype(jnp.bfloat16)
    above = jnp.where(r_id > c_id, 0.0, -1.0).astype(jnp.bfloat16)
    copies[0].wait()
    copies[3].wait()
    for i in range(nrow):
        piv8[i] = jnp.broadcast_to(piv[i : i + 1, :], piv8.shape[1:])

    def mask_block(b, carry):
        block = f_ref[b].T
        d = one(slots[b % nslot, b // nslot] == row + rows * (b // nslot)).astype(jnp.bfloat16)
        i, at = b // nslot, pl.ds(pl.multiple_of(b % nslot * f_ref.shape[1], f_ref.shape[1]), f_ref.shape[1])
        f2[i, at] = block + block * (d * below)
        f2[nrow + i, at] = block + block * (d * above)
        return carry

    lax.fori_loop(0, blocks, mask_block, 0, unroll=4)

    def row_sum(n, i, t):
        side = i if t is None else i + jnp.where(rlev[i] == TOP - t, nrow, 0)
        picked = [held[tbl[n * blocks + i * nslot + s]] for s in range(nslot)]
        return jnp.dot(jnp.concatenate(picked, axis=1), f2[side], preferred_element_type=jnp.float32)

    def part_copy(n, i):
        return pltpu.make_async_remote_copy(
            src_ref=psend.at[n, i], dst_ref=precv.at[n, col], send_sem=send1.at[n], recv_sem=recv1.at[n],
            device_id=(base + i, lane), device_id_type=MESH,
        )

    def parts(n, t, ready):
        sums = [row_sum(n, xc[dx][dc], t) for _, dx, dc in LINE]
        for (_, dx, dc), value in zip(LINE, sums):
            psend[n, xc[dx][dc]] = value.astype(jnp.bfloat16)
        ready()
        for _, dx, dc in LINE[:-1]:
            part_copy(n, xc[dx][dc]).start()

        @pl.when(off_diag)
        def _():
            part_copy(n, lane).start()

        @pl.when(on_diag)
        def _():
            precv[n, col] = psend[n, col]

    def wait_bytes(ref, count, sem):
        @pl.when(on_diag)
        def _():
            part = ref.at[pl.ds(0, count - 1)]
            pltpu.make_async_copy(part, part, sem).wait()

        @pl.when(off_diag)
        def _():
            part = ref.at[pl.ds(0, count)]
            pltpu.make_async_copy(part, part, sem).wait()

    def gathered(n):
        wait_bytes(precv.at[n], cols, recv1.at[n])
        return jnp.sum(precv[n].astype(jnp.float32), axis=0)

    def spread(n, value):
        land[n, own_pos] = value.astype(jnp.bfloat16)
        mine = land.at[n, own_pos]
        for dy, dx, dc in PLANE[:-1]:
            pltpu.make_async_remote_copy(
                src_ref=mine, dst_ref=mine, send_sem=send2.at[n], recv_sem=recv2.at[n],
                device_id=(ys[dy] + xc[dx][dc], col), device_id_type=MESH,
            ).start()

    def spread_wait(n):
        some = land.at[n, pl.ds(0, rows - 1)]
        pltpu.make_async_copy(some, some, recv2.at[n]).wait()
        held[pl.ds((n + 1) * ncol, ncol)] = land[n]

    def give_copy(d):
        return pltpu.make_async_remote_copy(
            src_ref=xs, dst_ref=xrecv.at[lane], send_sem=send3, recv_sem=recv3,
            device_id=(base + col, lax.rem(col + d, cols)), device_id_type=MESH,
        )

    def give():
        for d in zs:
            give_copy(d).start()

        @pl.when(off_diag)
        def _():
            give_copy(0).start()

        @pl.when(on_diag)
        def _():
            xrecv[lane] = xs[...]

    def piv_copy(to, i):
        return pltpu.make_async_remote_copy(
            src_ref=piv8.at[i], dst_ref=own_piv, send_sem=send5, recv_sem=recv5,
            device_id=(base + to, lane), device_id_type=MESH,
        )

    def pivots_start():
        @pl.when(on_diag)
        def _():
            for _, dx, dc in LINE[:-1]:
                piv_copy(xc[dx][dc], xc[dx][dc]).start()
            own_piv[...] = piv8[lane]

    def pivots_wait():
        @pl.when(on_diag)
        def _():
            some = piv8.at[pl.ds(0, cols - 1)]
            pltpu.make_async_copy(some, some, send5).wait()

        @pl.when(off_diag)
        def _():
            pltpu.make_async_copy(own_piv, own_piv, recv5).wait()

    n_in = jnp.where(on_diag, 2 * (cols - 1), 2 * cols) + rows - 1 + cols - 1

    def level_step(t, first):
        n = 2 * t
        parts(n, t, lambda: pl.semaphore_wait(barrier, n_in) if first else None)
        if first:
            pivots_start()
        sol = gathered(n)
        if first:
            pivots_wait()
        own = held[n * ncol + own_pos].astype(jnp.float32)
        sol = sol + (one(own_level == t) + one(own_level == TOP - t) * own_piv[0:1, :]) * own
        spread(n, sol)
        xs[0] += one(own_level == t) * sol
        xs[1] += one(own_level == TOP - t) * sol

        @pl.when(t == TOP - 1)
        def _():
            give()

        spread_wait(n)
        parts(n + 1, None, lambda: None)
        w = gathered(n + 1)
        rhs = one(own_level == t + 1) * low[mine_rows, :] + one(own_level == TOP - 1 - t) * up[mine_rows, :]
        spread(n + 1, rhs - w)
        spread_wait(n + 1)

    level_step(0, True)

    def body(t, carry):
        level_step(t, False)
        return carry

    lax.fori_loop(1, TOP, body, 0)

    n = ROUNDS - 1
    for i in range(nrow):
        own = held[n * ncol + row // cols + per * i].astype(jnp.float32)
        w = one(on_diag & (rlev[i] == TOP)) + one(on_diag & (rlev[i] == 0)) * piv8[i, 0:1, :]
        last[i] = (row_sum(n, i, TOP) + w * own).astype(jnp.bfloat16)
    zrecv[col] = last[...]
    for d in zs:
        pltpu.make_async_remote_copy(
            src_ref=last, dst_ref=zrecv.at[col], send_sem=send4, recv_sem=recv4,
            device_id=(row, lax.rem(col + d, cols)), device_id_type=MESH,
        ).start()

    def drain(m, carry):
        wait_bytes(psend.at[m], cols, send1.at[m])
        some = land.at[m, pl.ds(0, rows - 1)]
        pltpu.make_async_copy(some, some, send2.at[m]).wait()
        return carry

    lax.fori_loop(0, ROUNDS - 1, drain, 0)
    wait_bytes(xrecv, cols, recv3)
    wait_bytes(xrecv, cols, send3)
    some = zrecv.at[pl.ds(0, cols - 1)]
    pltpu.make_async_copy(some, some, recv4).wait()
    for i in range(nrow):
        sol = jnp.sum(zrecv[:, i].astype(jnp.float32), axis=0)
        lev = rlev[i]
        low_ref[:, i, :] = xrecv[i, 0] + one(lev == TOP) * sol
        up_ref[:, i, :] = xrecv[i, 1] + one(lev == 0) * sol
    pltpu.make_async_copy(some, some, send4).wait()


def shards(factor, inverse_pivot, lower_rhs, upper_rhs, snode_of_block, level_of_snode, slot_columns):
    rows, cols = lax.axis_size("row"), lax.axis_size("col")
    nrow, nslot, size = factor.shape[:3]
    nrhs, ncol = lower_rhs.shape[:2]
    f32, bf16 = jnp.float32, jnp.bfloat16
    blocks = nrow * nslot
    vmem = pl.BlockSpec(memory_space=pltpu.VMEM)
    hbm = pl.BlockSpec(memory_space=pltpu.HBM)
    dma = pltpu.SemaphoreType.DMA
    return pl.pallas_call(
        functools.partial(kernel, (rows, cols, nrow, nslot, ncol)),
        out_shape=[jax.ShapeDtypeStruct((nrhs, nrow, size), f32)] * 2,
        in_specs=[hbm] * 7,
        out_specs=[vmem, vmem],
        scratch_shapes=[
            pltpu.SMEM(snode_of_block.shape, jnp.int32),
            pltpu.SMEM(level_of_snode.shape, jnp.int32),
            pltpu.SMEM((nslot, nrow), jnp.int32),
            pltpu.SMEM((ROUNDS * blocks,), jnp.int32),
            pltpu.SMEM((nrow,), jnp.int32),
            pltpu.VMEM((blocks, size, size), bf16),
            pltpu.VMEM((nrhs * ncol, size), f32),
            pltpu.VMEM((nrhs * ncol, size), f32),
            pltpu.VMEM((nrow, size), f32),
            pltpu.VMEM((2 * nrow, nslot * size, size), bf16),
            pltpu.VMEM((nrow, 8, size), f32),
            pltpu.VMEM((8, size), f32),
            pltpu.VMEM((ROUNDS * ncol + 1, nrhs, size), bf16),
            pltpu.VMEM((ROUNDS - 1, ncol, nrhs, size), bf16),
            pltpu.VMEM((ROUNDS - 1, nrow, nrhs, size), bf16),
            pltpu.VMEM((ROUNDS - 1, cols, nrhs, size), bf16),
            pltpu.VMEM((2, nrhs, size), f32),
            pltpu.VMEM((nrow, 2, nrhs, size), f32),
            pltpu.VMEM((nrow, nrhs, size), bf16),
            pltpu.VMEM((cols, nrow, nrhs, size), bf16),
            dma((7,)),
            dma((ROUNDS - 1,)), dma((ROUNDS - 1,)), dma((ROUNDS - 1,)), dma((ROUNDS - 1,)),
            dma, dma, dma, dma, dma, dma,
        ],
        compiler_params=pltpu.CompilerParams(
            collective_id=0, has_side_effects=True, vmem_limit_bytes=VMEM_BYTES
        ),
        cost_estimate=pl.CostEstimate(
            flops=2 * ROUNDS * blocks * size * size * nrhs,
            bytes_accessed=4 * blocks * size * size, transcendentals=0,
        ),
    )(*[pltpu.with_memory_space_constraint(a, pltpu.HBM) for a in (
        snode_of_block, level_of_snode, slot_columns.T,
        factor.reshape(blocks, size, size), lower_rhs.reshape(nrhs * ncol, size),
        upper_rhs.reshape(nrhs * ncol, size), inverse_pivot,
    )])


def solution(mesh):
    in_specs = (
        P("row", "col", None, None),
        P("row", None),
        P(None, "col", None),
        P(None, "col", None),
        P(),
        P(),
        P("row", "col"),
    )
    out_specs = (P(None, "row", None), P(None, "row", None))
    return jax.shard_map(shards, mesh=mesh, in_specs=in_specs, out_specs=out_specs, check_vma=False)
```

```python
import functools

import jax
import jax.numpy as jnp
from jax import lax
from jax.experimental import pallas as pl
from jax.experimental.pallas import tpu as pltpu
from jax.sharding import PartitionSpec as P

MESH = pl.DeviceIdType.MESH
LEVELS = 6
TOP = LEVELS - 1
ROUNDS = 2 * LEVELS - 1
SIDE, CORES = 4, 2
FAR = 4096
VMEM_BYTES = 32 * 2**20


def ring(d, n):
    return min(d % n, -d % n)


PLANE = sorted(
    [(a, b, c) for a in range(SIDE) for b in range(SIDE) for c in range(CORES)],
    key=lambda o: (-ring(o[0], SIDE) - ring(o[1], SIDE), -o[2]),
)
LINE = [o for o in PLANE if o[0] == 0]


def kernel(
    dims, snode_hbm, level_hbm, slots_hbm, f_hbm, low_hbm, up_hbm, piv_hbm, out_ref,
    snode, level, slots, tbl, rlev, f_ref, low, up, piv, f2, piv8, own_piv, held, land, psend, precv, xs, xrecv, last, zrecv,
    sem_in, send1, recv1, send2, recv2, send3, recv3, send4, recv4, send5, recv5,
):
    rows, cols, nrow, nslot, ncol = dims
    nrhs = held.shape[1]
    per = rows // cols
    blocks = nrow * nslot
    total_blocks = rows * nrow
    zero = ROUNDS * ncol
    row, col = lax.axis_index("row"), lax.axis_index("col")
    y, x, core = row // (SIDE * CORES), row // CORES % SIDE, row % CORES
    base, lane = (row // cols) * cols, row % cols
    on_diag = col == lane
    off_diag = jnp.logical_not(on_diag)
    own_pos = row // cols + per * lane
    ys = [lax.rem(y + d, SIDE) * (SIDE * CORES) for d in range(SIDE)]
    xc = [[lax.rem(x + d, SIDE) * CORES + lax.rem(core + e, CORES) for e in range(CORES)] for d in range(SIDE)]
    zs = sorted(range(1, cols), key=lambda d: -ring(d, cols))

    barrier = pltpu.get_barrier_semaphore()

    def greet(to):
        pl.semaphore_signal(barrier, inc=1, device_id=to, device_id_type=MESH)

    for d in zs:
        greet((base + col, lax.rem(col + d, cols)))
    for _, dx, dc in LINE[:-1]:
        greet((base + xc[dx][dc], lane))

    @pl.when(off_diag)
    def _():
        greet((base + lane, lane))
        greet((base + col, col))

    copies = [
        pltpu.make_async_copy(src, dst, sem_in.at[k])
        for k, (src, dst) in enumerate([(f_hbm, f_ref), (low_hbm, low), (up_hbm, up), (piv_hbm, piv),
            (snode_hbm, snode), (level_hbm, level), (slots_hbm, slots)])
    ]
    for copy in copies:
        copy.start()

    for dy, dx, dc in PLANE[:-1]:
        greet((ys[dy] + xc[dx][dc], col))
    for d in zs:
        greet((row, lax.rem(col + d, cols)))

    for copy in copies[4:]:
        copy.wait()
    for i in range(nrow):
        rlev[i] = level[snode[row + rows * i]]

    own_level = level[snode[base + col + rows * lane]]

    def slot(b, carry):
        i = b // nslot
        this = row + rows * i
        lev, sn = rlev[i], snode[this]
        j = slots[b % nslot, i]
        valid = j < total_blocks
        jj = jnp.minimum(j, total_blocks - 1)
        j_sn = snode[jj]
        j_lev = level[j_sn]
        same = valid & (j_sn == sn)
        other = valid & (j_sn != sn)
        place = jj // cols
        lo_in = jnp.where((same & (j < this)) | (j == this), place, FAR)
        up_in = jnp.where((same & (j > this)) | (j == this), place, FAR)
        lo_out = jnp.where(other & (lev > j_lev), (2 * j_lev + 1) * ncol + place, zero)
        up_out = jnp.where(other & (lev < j_lev), (2 * (TOP - j_lev) + 1) * ncol + place, zero)
        for t in range(LEVELS):
            pick = jnp.where(lev == t, lo_in, jnp.where(lev == TOP - t, up_in, FAR))
            tbl[2 * t * blocks + b] = jnp.minimum(pick + 2 * t * ncol, zero)
            if t < TOP:
                pick = jnp.where(lev == t + 1, lo_out, jnp.where(lev == TOP - 1 - t, up_out, zero))
                tbl[(2 * t + 1) * blocks + b] = pick
        return carry

    lax.fori_loop(0, blocks, slot, 0)

    def one(flag):
        return jnp.where(flag, 1.0, 0.0).astype(jnp.float32)

    copies[1].wait()
    copies[2].wait()
    for j in range(ncol):
        lev = level[snode[j * cols + col]]
        rows_of = pl.ds(j, nrhs, stride=ncol)
        held[j] = (one(lev == 0) * low[rows_of, :] + one(lev == TOP) * up[rows_of, :]).astype(jnp.bfloat16)
    held[zero] = jnp.zeros(held.shape[1:], held.dtype)
    xs[...] = jnp.zeros_like(xs)
    mine_rows = pl.ds(own_pos, nrhs, stride=ncol)

    r_id = lax.broadcasted_iota(jnp.int32, f_ref.shape[1:], 0)
    c_id = lax.broadcasted_iota(jnp.int32, f_ref.shape[1:], 1)
    below = jnp.where(r_id < c_id, 0.0, -1.0).astype(jnp.bfloat16)
    above = jnp.where(r_id > c_id, 0.0, -1.0).astype(jnp.bfloat16)
    copies[0].wait()
    copies[3].wait()
    for i in range(nrow):
        piv8[i] = jnp.broadcast_to(piv[i : i + 1, :], piv8.shape[1:])

    def mask_block(b, carry):
        block = f_ref[b].T
        d = one(slots[b % nslot, b // nslot] == row + rows * (b // nslot)).astype(jnp.bfloat16)
        i, at = b // nslot, pl.ds(pl.multiple_of(b % nslot * f_ref.shape[1], f_ref.shape[1]), f_ref.shape[1])
        f2[i, at] = block + block * (d * below)
        f2[nrow + i, at] = block + block * (d * above)
        return carry

    lax.fori_loop(0, blocks, mask_block, 0, unroll=4)

    def row_sum(n, i, t):
        side = i if t is None else i + jnp.where(rlev[i] == TOP - t, nrow, 0)
        picked = [held[tbl[n * blocks + i * nslot + s]] for s in range(nslot)]
        return jnp.dot(jnp.concatenate(picked, axis=1), f2[side], preferred_element_type=jnp.float32)

    def part_copy(n, i):
        return pltpu.make_async_remote_copy(
            src_ref=psend.at[n, i], dst_ref=precv.at[n, col], send_sem=send1.at[n], recv_sem=recv1.at[n],
            device_id=(base + i, lane), device_id_type=MESH,
        )

    def parts(n, t, ready):
        sums = [row_sum(n, xc[dx][dc], t) for _, dx, dc in LINE]
        for (_, dx, dc), value in zip(LINE, sums):
            psend[n, xc[dx][dc]] = value.astype(jnp.bfloat16)
        ready()
        for _, dx, dc in LINE[:-1]:
            part_copy(n, xc[dx][dc]).start()

        @pl.when(off_diag)
        def _():
            part_copy(n, lane).start()

        @pl.when(on_diag)
        def _():
            precv[n, col] = psend[n, col]

    def wait_bytes(ref, count, sem):
        @pl.when(on_diag)
        def _():
            part = ref.at[pl.ds(0, count - 1)]
            pltpu.make_async_copy(part, part, sem).wait()

        @pl.when(off_diag)
        def _():
            part = ref.at[pl.ds(0, count)]
            pltpu.make_async_copy(part, part, sem).wait()

    def gathered(n):
        wait_bytes(precv.at[n], cols, recv1.at[n])
        return jnp.sum(precv[n].astype(jnp.float32), axis=0)

    def spread(n, value):
        land[n, own_pos] = value.astype(jnp.bfloat16)
        mine = land.at[n, own_pos]
        for dy, dx, dc in PLANE[:-1]:
            pltpu.make_async_remote_copy(
                src_ref=mine, dst_ref=mine, send_sem=send2.at[n], recv_sem=recv2.at[n],
                device_id=(ys[dy] + xc[dx][dc], col), device_id_type=MESH,
            ).start()

    def spread_wait(n):
        some = land.at[n, pl.ds(0, rows - 1)]
        pltpu.make_async_copy(some, some, recv2.at[n]).wait()
        held[pl.ds((n + 1) * ncol, ncol)] = land[n]

    def give_copy(d):
        return pltpu.make_async_remote_copy(
            src_ref=xs, dst_ref=xrecv.at[lane], send_sem=send3, recv_sem=recv3,
            device_id=(base + col, lax.rem(col + d, cols)), device_id_type=MESH,
        )

    def give():
        for d in zs:
            give_copy(d).start()

        @pl.when(off_diag)
        def _():
            give_copy(0).start()

        @pl.when(on_diag)
        def _():
            xrecv[lane] = xs[...]

    def piv_copy(to, i):
        return pltpu.make_async_remote_copy(
            src_ref=piv8.at[i], dst_ref=own_piv, send_sem=send5, recv_sem=recv5,
            device_id=(base + to, lane), device_id_type=MESH,
        )

    def pivots_start():
        @pl.when(on_diag)
        def _():
            for _, dx, dc in LINE[:-1]:
                piv_copy(xc[dx][dc], xc[dx][dc]).start()
            own_piv[...] = piv8[lane]

    def pivots_wait():
        @pl.when(on_diag)
        def _():
            some = piv8.at[pl.ds(0, cols - 1)]
            pltpu.make_async_copy(some, some, send5).wait()

        @pl.when(off_diag)
        def _():
            pltpu.make_async_copy(own_piv, own_piv, recv5).wait()

    n_in = jnp.where(on_diag, 2 * (cols - 1), 2 * cols) + rows - 1 + cols - 1

    def level_step(t, first):
        n = 2 * t
        parts(n, t, lambda: pl.semaphore_wait(barrier, n_in) if first else None)
        if first:
            pivots_start()
        sol = gathered(n)
        if first:
            pivots_wait()
        own = held[n * ncol + own_pos].astype(jnp.float32)
        sol = sol + (one(own_level == t) + one(own_level == TOP - t) * own_piv[0:1, :]) * own
        spread(n, sol)
        xs[0] += one(own_level == t) * sol
        xs[1] += one(own_level == TOP - t) * sol

        spread_wait(n)
        parts(n + 1, None, lambda: None)
        w = gathered(n + 1)
        rhs = one(own_level == t + 1) * low[mine_rows, :] + one(own_level == TOP - 1 - t) * up[mine_rows, :]
        spread(n + 1, rhs - w)

        @pl.when(t == TOP - 1)
        def _():
            give()

        spread_wait(n + 1)

    level_step(0, True)

    def body(t, carry):
        level_step(t, False)
        return carry

    lax.fori_loop(1, TOP, body, 0)

    n = ROUNDS - 1
    for i in range(nrow):
        own = held[n * ncol + row // cols + per * i].astype(jnp.float32)
        w = one(on_diag & (rlev[i] == TOP)) + one(on_diag & (rlev[i] == 0)) * piv8[i, 0:1, :]
        last[i] = (row_sum(n, i, TOP) + w * own).astype(jnp.bfloat16)
    zrecv[col] = last[...]
    for d in zs:
        pltpu.make_async_remote_copy(
            src_ref=last, dst_ref=zrecv.at[col], send_sem=send4, recv_sem=recv4,
            device_id=(row, lax.rem(col + d, cols)), device_id_type=MESH,
        ).start()

    def drain(m, carry):
        wait_bytes(psend.at[m], cols, send1.at[m])
        some = land.at[m, pl.ds(0, rows - 1)]
        pltpu.make_async_copy(some, some, send2.at[m]).wait()
        return carry

    lax.fori_loop(0, ROUNDS - 1, drain, 0)
    wait_bytes(xrecv, cols, recv3)
    wait_bytes(xrecv, cols, send3)
    some = zrecv.at[pl.ds(0, cols - 1)]
    pltpu.make_async_copy(some, some, recv4).wait()
    for i in range(nrow):
        sol = jnp.sum(zrecv[:, i].astype(jnp.float32), axis=0)
        lev = rlev[i]
        out_ref[0, :, i, :] = xrecv[i, 0] + one(lev == TOP) * sol
        out_ref[1, :, i, :] = xrecv[i, 1] + one(lev == 0) * sol
    pltpu.make_async_copy(some, some, send4).wait()


def shards(factor, inverse_pivot, lower_rhs, upper_rhs, snode_of_block, level_of_snode, slot_columns):
    rows, cols = lax.axis_size("row"), lax.axis_size("col")
    nrow, nslot, size = factor.shape[:3]
    nrhs, ncol = lower_rhs.shape[:2]
    f32, bf16 = jnp.float32, jnp.bfloat16
    blocks = nrow * nslot
    vmem = pl.BlockSpec(memory_space=pltpu.VMEM)
    hbm = pl.BlockSpec(memory_space=pltpu.HBM)
    dma = pltpu.SemaphoreType.DMA
    out = pl.pallas_call(
        functools.partial(kernel, (rows, cols, nrow, nslot, ncol)),
        out_shape=jax.ShapeDtypeStruct((2, nrhs, nrow, size), f32),
        in_specs=[hbm] * 7,
        out_specs=vmem,
        scratch_shapes=[
            pltpu.SMEM(snode_of_block.shape, jnp.int32),
            pltpu.SMEM(level_of_snode.shape, jnp.int32),
            pltpu.SMEM((nslot, nrow), jnp.int32),
            pltpu.SMEM((ROUNDS * blocks,), jnp.int32),
            pltpu.SMEM((nrow,), jnp.int32),
            pltpu.VMEM((blocks, size, size), bf16),
            pltpu.VMEM((nrhs * ncol, size), f32),
            pltpu.VMEM((nrhs * ncol, size), f32),
            pltpu.VMEM((nrow, size), f32),
            pltpu.VMEM((2 * nrow, nslot * size, size), bf16),
            pltpu.VMEM((nrow, 8, size), f32),
            pltpu.VMEM((8, size), f32),
            pltpu.VMEM((ROUNDS * ncol + 1, nrhs, size), bf16),
            pltpu.VMEM((ROUNDS - 1, ncol, nrhs, size), bf16),
            pltpu.VMEM((ROUNDS - 1, nrow, nrhs, size), bf16),
            pltpu.VMEM((ROUNDS - 1, cols, nrhs, size), bf16),
            pltpu.VMEM((2, nrhs, size), f32),
            pltpu.VMEM((nrow, 2, nrhs, size), f32),
            pltpu.VMEM((nrow, nrhs, size), bf16),
            pltpu.VMEM((cols, nrow, nrhs, size), bf16),
            dma((7,)),
            dma((ROUNDS - 1,)), dma((ROUNDS - 1,)), dma((ROUNDS - 1,)), dma((ROUNDS - 1,)),
            dma, dma, dma, dma, dma, dma,
        ],
        compiler_params=pltpu.CompilerParams(
            collective_id=0, has_side_effects=True, vmem_limit_bytes=VMEM_BYTES
        ),
        cost_estimate=pl.CostEstimate(
            flops=2 * ROUNDS * blocks * size * size * nrhs,
            bytes_accessed=4 * blocks * size * size, transcendentals=0,
        ),
    )(*[pltpu.with_memory_space_constraint(a, pltpu.HBM) for a in (
        snode_of_block, level_of_snode, slot_columns.T,
        factor.reshape(blocks, size, size), lower_rhs.reshape(nrhs * ncol, size),
        upper_rhs.reshape(nrhs * ncol, size), inverse_pivot,
    )])
    return out[0], out[1]


def solution(mesh):
    in_specs = (
        P("row", "col", None, None),
        P("row", None),
        P(None, "col", None),
        P(None, "col", None),
        P(),
        P(),
        P("row", "col"),
    )
    out_specs = (P(None, "row", None), P(None, "row", None))
    return jax.shard_map(shards, mesh=mesh, in_specs=in_specs, out_specs=out_specs, check_vma=False)
```

```python
import functools

import jax
import jax.numpy as jnp
from jax import lax
from jax.experimental import pallas as pl
from jax.experimental.pallas import tpu as pltpu
from jax.sharding import PartitionSpec as P

MESH = pl.DeviceIdType.MESH
LEVELS = 6
TOP = LEVELS - 1
ROUNDS = 2 * LEVELS - 1
SIDE, CORES = 4, 2
FAR = 4096
VMEM_BYTES = 32 * 2**20


def ring(d, n):
    return min(d % n, -d % n)


PLANE = sorted(
    [(a, b, c) for a in range(SIDE) for b in range(SIDE) for c in range(CORES)],
    key=lambda o: (-ring(o[0], SIDE) - ring(o[1], SIDE), -o[2]),
)
LINE = [o for o in PLANE if o[0] == 0]


def kernel(
    dims, snode_hbm, level_hbm, slots_hbm, f_hbm, low_hbm, up_hbm, piv_hbm, out_ref,
    snode, level, slots, tbl, rlev, f_ref, low, up, piv, f2, piv8, own_piv, held, land, psend, precv, xs, xrecv, last, zrecv,
    sem_in, send1, recv1, send2, recv2, send3, recv3, send4, recv4, send5, recv5,
):
    rows, cols, nrow, nslot, ncol = dims
    nrhs = held.shape[1]
    per = rows // cols
    blocks = nrow * nslot
    total_blocks = rows * nrow
    zero = ROUNDS * ncol
    row, col = lax.axis_index("row"), lax.axis_index("col")
    y, x, core = row // (SIDE * CORES), row // CORES % SIDE, row % CORES
    base, lane = (row // cols) * cols, row % cols
    on_diag = col == lane
    off_diag = jnp.logical_not(on_diag)
    own_pos = row // cols + per * lane
    ys = [lax.rem(y + d, SIDE) * (SIDE * CORES) for d in range(SIDE)]
    xc = [[lax.rem(x + d, SIDE) * CORES + lax.rem(core + e, CORES) for e in range(CORES)] for d in range(SIDE)]
    zs = sorted(range(1, cols), key=lambda d: -ring(d, cols))

    barrier = pltpu.get_barrier_semaphore()

    def greet(to):
        pl.semaphore_signal(barrier, inc=1, device_id=to, device_id_type=MESH)

    for d in zs:
        greet((base + col, lax.rem(col + d, cols)))
    for _, dx, dc in LINE[:-1]:
        greet((base + xc[dx][dc], lane))

    @pl.when(off_diag)
    def _():
        greet((base + lane, lane))
        greet((base + col, col))

    copies = [
        pltpu.make_async_copy(src, dst, sem_in.at[k])
        for k, (src, dst) in enumerate([(f_hbm, f_ref), (low_hbm, low), (up_hbm, up), (piv_hbm, piv),
            (snode_hbm, snode), (level_hbm, level), (slots_hbm, slots)])
    ]
    for copy in copies:
        copy.start()

    for dy, dx, dc in PLANE[:-1]:
        greet((ys[dy] + xc[dx][dc], col))
    for d in zs:
        greet((row, lax.rem(col + d, cols)))

    for copy in copies[4:]:
        copy.wait()
    for i in range(nrow):
        rlev[i] = level[snode[row + rows * i]]

    own_level = level[snode[base + col + rows * lane]]

    def slot(b, carry):
        i = b // nslot
        this = row + rows * i
        lev, sn = rlev[i], snode[this]
        j = slots[b % nslot, i]
        valid = j < total_blocks
        jj = jnp.minimum(j, total_blocks - 1)
        j_sn = snode[jj]
        j_lev = level[j_sn]
        same = valid & (j_sn == sn)
        other = valid & (j_sn != sn)
        place = jj // cols
        lo_in = jnp.where((same & (j < this)) | (j == this), place, FAR)
        up_in = jnp.where((same & (j > this)) | (j == this), place, FAR)
        lo_out = jnp.where(other & (lev > j_lev), (2 * j_lev + 1) * ncol + place, zero)
        up_out = jnp.where(other & (lev < j_lev), (2 * (TOP - j_lev) + 1) * ncol + place, zero)
        for t in range(LEVELS):
            pick = jnp.where(lev == t, lo_in, jnp.where(lev == TOP - t, up_in, FAR))
            tbl[2 * t * blocks + b] = jnp.minimum(pick + 2 * t * ncol, zero)
            if t < TOP:
                pick = jnp.where(lev == t + 1, lo_out, jnp.where(lev == TOP - 1 - t, up_out, zero))
                tbl[(2 * t + 1) * blocks + b] = pick
        return carry

    lax.fori_loop(0, blocks, slot, 0)

    def one(flag):
        return jnp.where(flag, 1.0, 0.0).astype(jnp.float32)

    copies[1].wait()
    copies[2].wait()
    for j in range(ncol):
        lev = level[snode[j * cols + col]]
        rows_of = pl.ds(j, nrhs, stride=ncol)
        held[j] = (one(lev == 0) * low[rows_of, :] + one(lev == TOP) * up[rows_of, :]).astype(jnp.bfloat16)
    held[zero] = jnp.zeros(held.shape[1:], held.dtype)
    xs[...] = jnp.zeros_like(xs)
    mine_rows = pl.ds(own_pos, nrhs, stride=ncol)

    r_id = lax.broadcasted_iota(jnp.int32, f_ref.shape[1:], 0)
    c_id = lax.broadcasted_iota(jnp.int32, f_ref.shape[1:], 1)
    below = jnp.where(r_id < c_id, 0.0, -1.0).astype(jnp.bfloat16)
    above = jnp.where(r_id > c_id, 0.0, -1.0).astype(jnp.bfloat16)
    copies[0].wait()
    copies[3].wait()
    for i in range(nrow):
        piv8[i] = jnp.broadcast_to(piv[i : i + 1, :], piv8.shape[1:])

    def mask_block(b, carry):
        block = f_ref[b].T
        d = one(slots[b % nslot, b // nslot] == row + rows * (b // nslot)).astype(jnp.bfloat16)
        i, at = b // nslot, pl.ds(pl.multiple_of(b % nslot * f_ref.shape[1], f_ref.shape[1]), f_ref.shape[1])
        f2[i, at] = block + block * (d * below)
        f2[nrow + i, at] = block + block * (d * above)
        return carry

    lax.fori_loop(0, blocks, mask_block, 0, unroll=4)

    def row_sum(n, i, t):
        side = i if t is None else i + jnp.where(rlev[i] == TOP - t, nrow, 0)
        picked = [held[tbl[n * blocks + i * nslot + s]] for s in range(nslot)]
        return jnp.dot(jnp.concatenate(picked, axis=1), f2[side], preferred_element_type=jnp.float32)

    def part_copy(n, i):
        return pltpu.make_async_remote_copy(
            src_ref=psend.at[n, i], dst_ref=precv.at[n, col], send_sem=send1.at[n], recv_sem=recv1.at[n],
            device_id=(base + i, lane), device_id_type=MESH,
        )

    def parts(n, t, ready):
        sums = [row_sum(n, xc[dx][dc], t) for _, dx, dc in LINE]
        for (_, dx, dc), value in zip(LINE, sums):
            psend[n, xc[dx][dc]] = value.astype(jnp.bfloat16)
        ready()
        for _, dx, dc in LINE[:-1]:
            part_copy(n, xc[dx][dc]).start()

        @pl.when(off_diag)
        def _():
            part_copy(n, lane).start()

        @pl.when(on_diag)
        def _():
            pltpu.make_async_copy(psend.at[n, col], precv.at[n, col], recv1.at[n]).start()

    def wait_bytes(ref, count, sem):
        @pl.when(on_diag)
        def _():
            part = ref.at[pl.ds(0, count - 1)]
            pltpu.make_async_copy(part, part, sem).wait()

        @pl.when(off_diag)
        def _():
            part = ref.at[pl.ds(0, count)]
            pltpu.make_async_copy(part, part, sem).wait()

    def gathered(n):
        pltpu.make_async_copy(precv.at[n], precv.at[n], recv1.at[n]).wait()
        return jnp.sum(precv[n].astype(jnp.float32), axis=0)

    def spread(n, value):
        land[n, own_pos] = value.astype(jnp.bfloat16)
        mine = land.at[n, own_pos]
        for dy, dx, dc in PLANE[:-1]:
            pltpu.make_async_remote_copy(
                src_ref=mine, dst_ref=mine, send_sem=send2.at[n], recv_sem=recv2.at[n],
                device_id=(ys[dy] + xc[dx][dc], col), device_id_type=MESH,
            ).start()

    def spread_wait(n):
        some = land.at[n, pl.ds(0, rows - 1)]
        pltpu.make_async_copy(some, some, recv2.at[n]).wait()
        held[pl.ds((n + 1) * ncol, ncol)] = land[n]

    def give_copy(d):
        return pltpu.make_async_remote_copy(
            src_ref=xs, dst_ref=xrecv.at[lane], send_sem=send3, recv_sem=recv3,
            device_id=(base + col, lax.rem(col + d, cols)), device_id_type=MESH,
        )

    def give():
        for d in zs:
            give_copy(d).start()

        @pl.when(off_diag)
        def _():
            give_copy(0).start()

        @pl.when(on_diag)
        def _():
            xrecv[lane] = xs[...]

    def piv_copy(to, i):
        return pltpu.make_async_remote_copy(
            src_ref=piv8.at[i], dst_ref=own_piv, send_sem=send5, recv_sem=recv5,
            device_id=(base + to, lane), device_id_type=MESH,
        )

    def pivots_start():
        @pl.when(on_diag)
        def _():
            for _, dx, dc in LINE[:-1]:
                piv_copy(xc[dx][dc], xc[dx][dc]).start()
            own_piv[...] = piv8[lane]

    def pivots_wait():
        @pl.when(on_diag)
        def _():
            some = piv8.at[pl.ds(0, cols - 1)]
            pltpu.make_async_copy(some, some, send5).wait()

        @pl.when(off_diag)
        def _():
            pltpu.make_async_copy(own_piv, own_piv, recv5).wait()

    n_in = jnp.where(on_diag, 2 * (cols - 1), 2 * cols) + rows - 1 + cols - 1

    def level_step(t, first):
        n = 2 * t
        parts(n, t, lambda: pl.semaphore_wait(barrier, n_in) if first else None)
        if first:
            pivots_start()
        sol = gathered(n)
        if first:
            pivots_wait()
        own = held[n * ncol + own_pos].astype(jnp.float32)
        sol = sol + (one(own_level == t) + one(own_level == TOP - t) * own_piv[0:1, :]) * own
        spread(n, sol)
        xs[0] += one(own_level == t) * sol
        xs[1] += one(own_level == TOP - t) * sol

        spread_wait(n)
        parts(n + 1, None, lambda: None)
        w = gathered(n + 1)
        rhs = one(own_level == t + 1) * low[mine_rows, :] + one(own_level == TOP - 1 - t) * up[mine_rows, :]
        spread(n + 1, rhs - w)

        @pl.when(t == TOP - 1)
        def _():
            give()

        spread_wait(n + 1)

    level_step(0, True)

    def body(t, carry):
        level_step(t, False)
        return carry

    lax.fori_loop(1, TOP, body, 0)

    n = ROUNDS - 1
    for i in range(nrow):
        own = held[n * ncol + row // cols + per * i].astype(jnp.float32)
        w = one(on_diag & (rlev[i] == TOP)) + one(on_diag & (rlev[i] == 0)) * piv8[i, 0:1, :]
        last[i] = (row_sum(n, i, TOP) + w * own).astype(jnp.bfloat16)
    zrecv[col] = last[...]
    for d in zs:
        pltpu.make_async_remote_copy(
            src_ref=last, dst_ref=zrecv.at[col], send_sem=send4, recv_sem=recv4,
            device_id=(row, lax.rem(col + d, cols)), device_id_type=MESH,
        ).start()

    def drain(m, carry):
        wait_bytes(psend.at[m], cols, send1.at[m])
        some = land.at[m, pl.ds(0, rows - 1)]
        pltpu.make_async_copy(some, some, send2.at[m]).wait()
        return carry

    lax.fori_loop(0, ROUNDS - 1, drain, 0)
    wait_bytes(xrecv, cols, recv3)
    wait_bytes(xrecv, cols, send3)
    some = zrecv.at[pl.ds(0, cols - 1)]
    pltpu.make_async_copy(some, some, recv4).wait()
    for i in range(nrow):
        sol = jnp.sum(zrecv[:, i].astype(jnp.float32), axis=0)
        lev = rlev[i]
        out_ref[0, :, i, :] = xrecv[i, 0] + one(lev == TOP) * sol
        out_ref[1, :, i, :] = xrecv[i, 1] + one(lev == 0) * sol
    pltpu.make_async_copy(some, some, send4).wait()


def shards(factor, inverse_pivot, lower_rhs, upper_rhs, snode_of_block, level_of_snode, slot_columns):
    rows, cols = lax.axis_size("row"), lax.axis_size("col")
    nrow, nslot, size = factor.shape[:3]
    nrhs, ncol = lower_rhs.shape[:2]
    f32, bf16 = jnp.float32, jnp.bfloat16
    blocks = nrow * nslot
    vmem = pl.BlockSpec(memory_space=pltpu.VMEM)
    hbm = pl.BlockSpec(memory_space=pltpu.HBM)
    dma = pltpu.SemaphoreType.DMA
    out = pl.pallas_call(
        functools.partial(kernel, (rows, cols, nrow, nslot, ncol)),
        out_shape=jax.ShapeDtypeStruct((2, nrhs, nrow, size), f32),
        in_specs=[hbm] * 7,
        out_specs=vmem,
        scratch_shapes=[
            pltpu.SMEM(snode_of_block.shape, jnp.int32),
            pltpu.SMEM(level_of_snode.shape, jnp.int32),
            pltpu.SMEM((nslot, nrow), jnp.int32),
            pltpu.SMEM((ROUNDS * blocks,), jnp.int32),
            pltpu.SMEM((nrow,), jnp.int32),
            pltpu.VMEM((blocks, size, size), bf16),
            pltpu.VMEM((nrhs * ncol, size), f32),
            pltpu.VMEM((nrhs * ncol, size), f32),
            pltpu.VMEM((nrow, size), f32),
            pltpu.VMEM((2 * nrow, nslot * size, size), bf16),
            pltpu.VMEM((nrow, 8, size), f32),
            pltpu.VMEM((8, size), f32),
            pltpu.VMEM((ROUNDS * ncol + 1, nrhs, size), bf16),
            pltpu.VMEM((ROUNDS - 1, ncol, nrhs, size), bf16),
            pltpu.VMEM((ROUNDS - 1, nrow, nrhs, size), bf16),
            pltpu.VMEM((ROUNDS - 1, cols, nrhs, size), bf16),
            pltpu.VMEM((2, nrhs, size), f32),
            pltpu.VMEM((nrow, 2, nrhs, size), f32),
            pltpu.VMEM((nrow, nrhs, size), bf16),
            pltpu.VMEM((cols, nrow, nrhs, size), bf16),
            dma((7,)),
            dma((ROUNDS - 1,)), dma((ROUNDS - 1,)), dma((ROUNDS - 1,)), dma((ROUNDS - 1,)),
            dma, dma, dma, dma, dma, dma,
        ],
        compiler_params=pltpu.CompilerParams(
            collective_id=0, has_side_effects=True, vmem_limit_bytes=VMEM_BYTES
        ),
        cost_estimate=pl.CostEstimate(
            flops=2 * ROUNDS * blocks * size * size * nrhs,
            bytes_accessed=4 * blocks * size * size, transcendentals=0,
        ),
    )(*[pltpu.with_memory_space_constraint(a, pltpu.HBM) for a in (
        snode_of_block, level_of_snode, slot_columns.T,
        factor.reshape(blocks, size, size), lower_rhs.reshape(nrhs * ncol, size),
        upper_rhs.reshape(nrhs * ncol, size), inverse_pivot,
    )])
    return out[0], out[1]


def solution(mesh):
    in_specs = (
        P("row", "col", None, None),
        P("row", None),
        P(None, "col", None),
        P(None, "col", None),
        P(),
        P(),
        P("row", "col"),
    )
    out_specs = (P(None, "row", None), P(None, "row", None))
    return jax.shard_map(shards, mesh=mesh, in_specs=in_specs, out_specs=out_specs, check_vma=False)
```
